32 devices in a mesh: cells: 4 (over z), grow: 4 (over x, core), gcol: 2 (over y).
Axes of the slice: x: 2, y: 2, z: 4, core: 2. Of those that a mesh axis runs over, the one named last changes fastest.
Arguments:
- counts: int32 [4608, 4, 2, 1024], P('cells', 'grow', 'gcol'), may hold values from 0 to 2689, as said below
- gene_mean: float32 [4, 2, 1024], P('grow', 'gcol'), may hold values from 0.2 to 1.2
- gene_scale: float32 [4, 2, 1024], P('grow', 'gcol'), may hold values from 0.4 to 2
Outputs:
- coexpression: float32 [4, 2048, 2, 4, 1024], P('grow', 'cells', 'gcol')
The draws below stay inside these ranges and needn't reach their ends.
Inputs may be any that keep to these rules, and one draw needn't show every extreme that they name: `counts`: every cell has at least one count.
All inputs are finite; a program needn't handle non-finite values.
Results may differ from the reference program's by a relative error of at most 0.0008.
Values may be sent and summed in bfloat16 or wider, within the bound.
A program may use at most 384 MiB of HBM per device.

```python
import math
import jax
import jax.numpy as jnp
from jax import lax

GENES = 8192
CELLS = 4608
SPAN = 1024
N_GROW = 4
N_GCOL = 2


def draw_counts(key, part):
    key = jax.random.fold_in(key, 11)
    key_cell, key_gene, key_value, key_pick, key_load, key_first, key_second = jax.random.split(key, 7)
    programs = max(GENES // 8, 4)
    cell_shift = jax.random.randint(key_cell, (CELLS,), 0, 5)
    cell_shift = cell_shift.at[0].set(4)
    gene_shift = jax.random.randint(key_gene, (GENES,), 0, 4)
    gene_shift = gene_shift.at[GENES - 1].set(3)
    genes = jnp.arange(GENES, dtype=jnp.int32)
    ramp = 1 + 3 * genes // GENES
    first = jax.random.randint(key_first, (GENES,), 0, programs)
    second = jax.random.randint(key_second, (GENES,), 0, programs)
    loading = jax.random.randint(key_load, (CELLS, programs), 0, 4)
    loading = loading.at[0, first[GENES - 1]].set(3)
    loading = loading.at[0, second[GENES - 1]].set(3)
    activity = 1 + jnp.take(loading, first, axis=1) + jnp.take(loading, second, axis=1)
    cell_level = jnp.left_shift(jnp.int32(1), cell_shift)
    gene_level = jnp.left_shift(jnp.int32(1), gene_shift) * ramp
    upper = cell_level[:, None] * gene_level[None, :] * activity
    values = jax.random.randint(key_value, (CELLS, GENES), 0, upper + 1)
    values = values.at[0, GENES - 1].set(upper[0, GENES - 1])
    picked = jax.random.randint(key_pick, (CELLS,), 0, GENES)
    picked = picked.at[0].set(GENES - 1)
    values = values + (genes[None, :] == picked[:, None]).astype(jnp.int32)
    return values.reshape(CELLS, N_GROW, N_GCOL, GENES // (N_GROW * N_GCOL)).astype(jnp.int32)


def levels(rng, shape, cuts, least, top_value):
    factor_of, own = 1.0, jax.random.fold_in(rng, 6)
    for dim, blocks in cuts:
        draws = jnp.exp(jax.random.uniform(jax.random.fold_in(own, dim), (blocks,), jnp.float32, least / len(cuts), top_value / len(cuts)))
        factor_of = factor_of * jnp.repeat(draws, shape[dim] // blocks).reshape([-1 if axis == dim else 1 for axis in range(len(shape))])
    return factor_of


def setup_inputs(seed: int = 0) -> dict:
    seeds = jax.random.split(jax.random.key(seed), 4)
    counts = draw_counts(jax.random.fold_in(seeds[3], 71), 0)
    gene_mean = jnp.clip(0.2 + 1 * jax.random.uniform(seeds[1], (N_GROW, N_GCOL, SPAN), jnp.float32) ** levels(seeds[1], (N_GROW, N_GCOL, SPAN), ((0, 4), (1, 2)), -0.2, 0.2), 0.2, 1.2)
    gene_scale = jnp.clip(jnp.exp(math.log(2.0) - 1.609438 * jax.random.uniform(seeds[2], (N_GROW, N_GCOL, SPAN), jnp.float32) ** levels(seeds[2], (N_GROW, N_GCOL, SPAN), ((0, 4), (1, 2)), -0.2, 0.2)), 0.4, 2.0)
    return {"counts": counts, "gene_mean": gene_mean, "gene_scale": gene_scale}


def reference(counts, gene_mean, gene_scale):
    flat = counts.reshape(CELLS, GENES).astype(jnp.float32)
    totals = jnp.sum(flat, axis=1)
    lognorm = jnp.log1p(flat * GENES / totals[:, None])
    standard = ((lognorm - gene_mean.reshape(GENES)[None, :]) / gene_scale.reshape(GENES)[None, :]).astype(jnp.bfloat16)
    values = standard.astype(jnp.float32)
    gram = lax.dot_general(values, values, (((0,), (0,)), ((), ())), precision=lax.Precision.HIGHEST, preferred_element_type=jnp.float32)
    gram = gram / CELLS
    gram = gram.reshape(GENES, N_GROW, N_GCOL, SPAN).transpose(0, 2, 1, 3)
    return gram.reshape(N_GROW, GENES // N_GROW, N_GCOL, N_GROW, SPAN)
```

```python
import functools

import jax
import jax.numpy as jnp
from jax import lax
from jax.experimental import pallas as pl
from jax.experimental.pallas import tpu as pltpu
from jax.sharding import PartitionSpec as P

GENES = 8192
MESH = pl.DeviceIdType.MESH
SIB, UP, DOWN, ACROSS = range(4)
TILE = 256


def standardize(counts, gene_mean, gene_scale):
    cell_rows, width = counts.shape[0], counts.shape[3]
    local = counts.reshape(cell_rows, width).astype(jnp.float32)
    totals = lax.psum(jnp.sum(local, axis=1), ("grow", "gcol"))
    lognorm = jnp.log1p(local * GENES / totals[:, None])
    return ((lognorm - gene_mean.reshape(1, width)) / gene_scale.reshape(1, width)).astype(
        jnp.bfloat16
    )


def gram_kernel(nz, rows, cuts, std_ref, out_ref, xs, landed, turned, acc,
                load_sem, recv_sem, send_sem, rows_recv, rows_send, out_sem):
    zi, gi, yi = lax.axis_index("cells"), lax.axis_index("grow"), lax.axis_index("gcol")
    width = xs.shape[3]
    last = nz - 1
    x, c = gi // 2, gi % 2
    g_sib = x * 2 + (1 - c)
    g_across = (1 - x) * 2 + c
    target = {
        SIB: {"grow": g_sib},
        UP: {"cells": jnp.minimum(zi + 1, last)},
        DOWN: {"cells": jnp.maximum(zi - 1, 0)},
        ACROSS: {"grow": g_across},
    }
    owner = (zi * 2) // nz == yi
    own_col = pl.multiple_of((zi % (nz // 2)) * rows, rows)

    barrier = pltpu.get_barrier_semaphore()

    def greet(to):
        pl.semaphore_signal(barrier, inc=1, device_id=to, device_id_type=MESH)

    greet(target[SIB])
    greet(target[ACROSS])
    greet({"gcol": 1 - yi})
    pl.when(zi < last)(lambda: greet(target[UP]))
    pl.when(zi > 0)(lambda: greet(target[DOWN]))
    load = pltpu.make_async_copy(std_ref, xs.at[zi, gi], load_sem)
    load.start()
    ends_of_line = (zi == 0).astype(jnp.int32) + (zi == last).astype(jnp.int32)
    pl.semaphore_wait(barrier, 5 - ends_of_line)

    def part(h):
        return pl.ds(cuts[h], cuts[h + 1] - cuts[h])

    def copy(kind, z, g, h):
        ref = xs.at[z, g, part(h), :]
        return pltpu.make_async_remote_copy(
            src_ref=ref, dst_ref=ref,
            send_sem=send_sem.at[kind, z, g // 2, h], recv_sem=recv_sem.at[z, g, h],
            device_id=target[kind], device_id_type=MESH,
        )

    def rows_copy(z, h):
        return pltpu.make_async_remote_copy(
            src_ref=xs.at[z, gi, part(h), pl.ds(own_col, rows)], dst_ref=landed.at[z, part(h), :],
            send_sem=rows_send.at[z, h], recv_sem=rows_recv.at[z, h],
            device_id={"gcol": 1 - yi}, device_id_type=MESH,
        )

    def sends(z, mine, h, act):
        g = gi if mine else g_across
        if mine:
            pl.when((z <= zi) & (zi < last))(lambda: act(copy(UP, z, g, h)))
            pl.when((z >= zi) & (zi > 0))(lambda: act(copy(DOWN, z, g, h)))
            if h == 0:
                act(copy(ACROSS, z, g, h))
            else:
                by_line = ((z == 0) & (zi != 0)) | ((z == last) & (zi != last))
                pl.when(jnp.logical_not(by_line))(lambda: act(copy(ACROSS, z, g, h)))
            pl.when(owner)(lambda: act(rows_copy(z, h)))
        elif h == 1:
            pl.when((z == 0) & (zi < last))(lambda: act(copy(UP, z, g, h)))
            pl.when((z == last) & (zi > 0))(lambda: act(copy(DOWN, z, g, h)))
        act(copy(SIB, z, g, h))

    def start(dma):
        dma.start()

    def finish(dma):
        dma.wait_send()

    def arrive(z, g, h):
        copy(SIB, z, g, h).wait_recv()

    def place(d, side):
        z = zi - d + 2 * d * side
        valid = (z >= 0) & (z <= last) & ((d > 0) | (side == 0))
        return z, valid

    def forward(d):
        for h in range(2):
            for side in range(2):
                z, valid = place(d, side)

                @pl.when(valid)
                def _():
                    pl.when(d > 0)(lambda: arrive(z, gi, h))
                    sends(z, True, h, start)

    def ends(d):
        for z, hit in ((0, zi == d - 1), (last, last - zi == d - 1)):
            @pl.when(hit)
            def _():
                arrive(z, g_across, 1)
                sends(z, False, 1, start)

    def turn(z, h):
        for k in range(cuts[h], cuts[h + 1], 128):
            @pl.when(owner)
            def _():
                turned[z, :, k:k + 128] = xs[z, gi, k:k + 128, pl.ds(own_col, rows)].T

            @pl.when(jnp.logical_not(owner))
            def _():
                turned[z, :, k:k + 128] = landed[z, k:k + 128, :].T

    def multiply(z, g, h):
        tiles = width // TILE

        def body(i, carry):
            a = (g // 2) * 2 + i // tiles
            n = pl.ds(pl.multiple_of((i % tiles) * TILE, TILE), TILE)
            acc[a, :, n] += jnp.dot(
                turned[z, :, part(h)], xs[z, a, part(h), n], preferred_element_type=jnp.float32
            )
            return carry

        lax.fori_loop(0, 2 * tiles, body, 0)

    def near(d):
        def body(side, carry):
            z, valid = place(d, side)

            @pl.when(valid)
            def _():
                for h in range(2):
                    pl.when(jnp.logical_not(owner))(lambda: rows_copy(z, h).wait_recv())
                    turn(z, h)
                    arrive(z, g_sib, h)
                    multiply(z, gi, h)
            return carry

        lax.fori_loop(0, 2, body, 0)

    def far(d):
        def body(side, carry):
            z, valid = place(d, side)

            @pl.when(valid)
            def _():
                for h in range(2):
                    def take():
                        arrive(z, g_across, h)
                        start(copy(SIB, z, g_across, h))
                    if h == 0:
                        take()
                    else:
                        pl.when((z > 0) & (z < last))(take)
                    arrive(z, (1 - x) * 2 + (1 - c), h)
                    multiply(z, g_across, h)
            return carry

        lax.fori_loop(0, 2, body, 0)

    acc[...] = jnp.zeros_like(acc)
    load.wait()

    def step(d, carry):
        pl.when(d < nz)(lambda: forward(d))
        ends(d)
        pl.when(d < nz)(lambda: near(d))
        pl.when(d > 0)(lambda: far(d - 1))
        return carry

    lax.fori_loop(0, nz + 1, step, 0)

    outs = [
        pltpu.make_async_copy(acc.at[a], out_ref.at[:, a, :], out_sem.at[a])
        for a in range(acc.shape[0])
    ]
    for dma in outs:
        dma.start()

    def drain(z, carry):
        for h in range(2):
            for mine in (True, False):
                sends(z, mine, h, finish)
        return carry

    lax.fori_loop(0, nz, drain, 0)
    for dma in outs:
        dma.wait()


def line_plan(counts, gene_mean, gene_scale):
    nz, n_grow = lax.axis_size("cells"), lax.axis_size("grow")
    cell_rows, width = counts.shape[0], counts.shape[3]
    standard = standardize(counts, gene_mean, gene_scale)
    rows = 2 * width // nz
    cuts = (0, -(-cell_rows // 256) * 128, cell_rows)
    flops = 2 * rows * n_grow * width * nz * cell_rows
    summed = pl.pallas_call(
        functools.partial(gram_kernel, nz, rows, cuts),
        out_shape=jax.ShapeDtypeStruct((rows, n_grow, width), jnp.float32),
        in_specs=[pl.BlockSpec(memory_space=pl.ANY)],
        out_specs=pl.BlockSpec(memory_space=pl.ANY),
        scratch_shapes=[
            pltpu.VMEM((nz, n_grow, cell_rows, width), jnp.bfloat16),
            pltpu.VMEM((nz, cell_rows, rows), jnp.bfloat16),
            pltpu.VMEM((nz, rows, cell_rows), jnp.bfloat16),
            pltpu.VMEM((n_grow, rows, width), jnp.float32),
            pltpu.SemaphoreType.DMA,
            pltpu.SemaphoreType.DMA((nz, n_grow, 2)),
            pltpu.SemaphoreType.DMA((4, nz, 2, 2)),
            pltpu.SemaphoreType.DMA((nz, 2)),
            pltpu.SemaphoreType.DMA((nz, 2)),
            pltpu.SemaphoreType.DMA((n_grow,)),
        ],
        compiler_params=pltpu.CompilerParams(
            collective_id=0, has_side_effects=True, vmem_limit_bytes=60 * 2**20
        ),
        cost_estimate=pl.CostEstimate(
            flops=flops, bytes_accessed=4 * rows * n_grow * width, transcendentals=0
        ),
    )(standard)
    return (summed / (nz * cell_rows)).reshape(1, rows, 1, n_grow, width)


def sum_plan(counts, gene_mean, gene_scale):
    cell_rows, width = counts.shape[0], counts.shape[3]
    standard = standardize(counts, gene_mean, gene_scale).reshape(cell_rows, 1, width)
    n_grow, n_gcol, n_cells = (lax.axis_size(a) for a in ("grow", "gcol", "cells"))
    row_flat = lax.all_gather(standard, "gcol", axis=1, tiled=True).reshape(cell_rows, -1)
    col_flat = lax.all_gather(standard, "grow", axis=1, tiled=True).reshape(cell_rows, -1)
    owned = row_flat.shape[1] // n_cells
    summed = lax.psum_scatter(
        lax.dot_general(
            row_flat, col_flat, (((0,), (0,)), ((), ())), preferred_element_type=jnp.float32
        ),
        "cells",
        scatter_dimension=0,
        tiled=True,
    )
    return (summed / (n_cells * cell_rows)).reshape(1, owned, 1, n_grow, width)


def solution(mesh):
    placed = (P("cells", "grow", "gcol", None), P("grow", "gcol", None), P("grow", "gcol", None))
    sizes = tuple(mesh.shape[a] for a in ("cells", "grow", "gcol"))
    return jax.shard_map(
        line_plan if sizes == (4, 4, 2) else sum_plan,
        mesh=mesh,
        in_specs=placed,
        out_specs=P("grow", "cells", "gcol", None, None),
        check_vma=False,
    )
```

```python
import functools

import jax
import jax.numpy as jnp
from jax import lax
from jax.experimental import pallas as pl
from jax.experimental.pallas import tpu as pltpu
from jax.sharding import PartitionSpec as P

GENES = 8192
MESH = pl.DeviceIdType.MESH
SIB, UP, DOWN, ACROSS = range(4)
TILE = 256


def standardize(counts, gene_mean, gene_scale):
    cell_rows, width = counts.shape[0], counts.shape[3]
    local = counts.reshape(cell_rows, width).astype(jnp.float32)
    totals = lax.psum(jnp.sum(local, axis=1), ("grow", "gcol"))
    lognorm = jnp.log1p(local * GENES / totals[:, None])
    return ((lognorm - gene_mean.reshape(1, width)) / gene_scale.reshape(1, width)).astype(
        jnp.bfloat16
    )


def gram_kernel(nz, rows, cuts, counts_ref, mean_ref, scale_ref, out_ref,
                staged, sums, heard, xs, landed, turned, acc,
                load_sem, sums_recv, sums_send, recv_sem, send_sem, rows_recv, rows_send, out_sem):
    zi, gi, yi = lax.axis_index("cells"), lax.axis_index("grow"), lax.axis_index("gcol")
    width = xs.shape[3]
    last = nz - 1
    x, c = gi // 2, gi % 2
    g_sib = x * 2 + (1 - c)
    g_across = (1 - x) * 2 + c
    target = {
        SIB: {"grow": g_sib},
        UP: {"cells": jnp.minimum(zi + 1, last)},
        DOWN: {"cells": jnp.maximum(zi - 1, 0)},
        ACROSS: {"grow": g_across},
    }
    owner = (zi * 2) // nz == yi
    own_col = pl.multiple_of((zi % (nz // 2)) * rows, rows)

    barrier = pltpu.get_barrier_semaphore()

    def greet(to):
        pl.semaphore_signal(barrier, inc=1, device_id=to, device_id_type=MESH)

    peers = [
        {"grow": (gi + dg) % 4, "gcol": (yi + dy) % 2}
        for dg in range(4) for dy in range(2) if dg or dy
    ]
    for peer in peers:
        greet(peer)
    pl.when(zi < last)(lambda: greet(target[UP]))
    pl.when(zi > 0)(lambda: greet(target[DOWN]))
    loads = [
        pltpu.make_async_copy(
            counts_ref.at[pl.ds(cuts[h], cuts[h + 1] - cuts[h]), 0, :],
            staged.at[pl.ds(cuts[h], cuts[h + 1] - cuts[h]), :], load_sem.at[h],
        )
        for h in range(2)
    ]
    for dma in loads:
        dma.start()

    def part(h):
        return pl.ds(cuts[h], cuts[h + 1] - cuts[h])

    def copy(kind, z, g, h):
        ref = xs.at[z, g, part(h), :]
        return pltpu.make_async_remote_copy(
            src_ref=ref, dst_ref=ref,
            send_sem=send_sem.at[kind, z, g // 2, h], recv_sem=recv_sem.at[z, g, h],
            device_id=target[kind], device_id_type=MESH,
        )

    def rows_copy(z, h):
        return pltpu.make_async_remote_copy(
            src_ref=xs.at[z, gi, part(h), pl.ds(own_col, rows)], dst_ref=landed.at[z, part(h), :],
            send_sem=rows_send.at[z, h], recv_sem=rows_recv.at[z, h],
            device_id={"gcol": 1 - yi}, device_id_type=MESH,
        )

    def sends(z, mine, h, act):
        g = gi if mine else g_across
        if mine:
            pl.when((z <= zi) & (zi < last))(lambda: act(copy(UP, z, g, h)))
            pl.when((z >= zi) & (zi > 0))(lambda: act(copy(DOWN, z, g, h)))
            if h == 0:
                act(copy(ACROSS, z, g, h))
            else:
                by_line = ((z == 0) & (zi != 0)) | ((z == last) & (zi != last))
                pl.when(jnp.logical_not(by_line))(lambda: act(copy(ACROSS, z, g, h)))
            pl.when(owner)(lambda: act(rows_copy(z, h)))
        elif h == 1:
            pl.when((z == 0) & (zi < last))(lambda: act(copy(UP, z, g, h)))
            pl.when((z == last) & (zi > 0))(lambda: act(copy(DOWN, z, g, h)))
        act(copy(SIB, z, g, h))

    def start(dma):
        dma.start()

    def finish(dma):
        dma.wait_send()

    def arrive(z, g, h):
        copy(SIB, z, g, h).wait_recv()

    def place(d, side):
        z = zi - d + 2 * d * side
        valid = (z >= 0) & (z <= last) & ((d > 0) | (side == 0))
        return z, valid

    def forward(d):
        for h in range(2):
            for side in range(2):
                z, valid = place(d, side)

                @pl.when(valid)
                def _():
                    pl.when(d > 0)(lambda: arrive(z, gi, h))
                    sends(z, True, h, start)

    def ends(d):
        for z, hit in ((0, zi == d - 1), (last, last - zi == d - 1)):
            @pl.when(hit)
            def _():
                arrive(z, g_across, 1)
                sends(z, False, 1, start)

    def turn(z, h):
        for k in range(cuts[h], cuts[h + 1], 128):
            @pl.when(owner)
            def _():
                turned[z, :, k:k + 128] = xs[z, gi, k:k + 128, pl.ds(own_col, rows)].T

            @pl.when(jnp.logical_not(owner))
            def _():
                turned[z, :, k:k + 128] = landed[z, k:k + 128, :].T

    def multiply(z, g, h):
        tiles = width // TILE

        def body(i, carry):
            a = (g // 2) * 2 + i // tiles
            n = pl.ds(pl.multiple_of((i % tiles) * TILE, TILE), TILE)
            acc[a, :, n] += jnp.dot(
                turned[z, :, part(h)], xs[z, a, part(h), n], preferred_element_type=jnp.float32
            )
            return carry

        lax.fori_loop(0, 2 * tiles, body, 0)

    def near(d):
        def body(side, carry):
            z, valid = place(d, side)

            @pl.when(valid)
            def _():
                for h in range(2):
                    pl.when(jnp.logical_not(owner))(lambda: rows_copy(z, h).wait_recv())
                    turn(z, h)
                    arrive(z, g_sib, h)
                    multiply(z, gi, h)
            return carry

        lax.fori_loop(0, 2, body, 0)

    def far(d):
        def body(side, carry):
            z, valid = place(d, side)

            def take(h):
                arrive(z, g_across, h)
                start(copy(SIB, z, g_across, h))

            def use(h):
                arrive(z, (1 - x) * 2 + (1 - c), h)
                multiply(z, g_across, h)

            at_end = (z == 0) | (z == last)

            @pl.when(valid)
            def _():
                pl.when(at_end)(lambda: use(1))
                take(0)
                use(0)

                @pl.when(jnp.logical_not(at_end))
                def _():
                    take(1)
                    use(1)
            return carry

        lax.fori_loop(0, 2, body, 0)

    def add_up(k, carry):
        r = pl.ds(pl.multiple_of(k * 128, 128), 128)
        total = staged[r, 0:128].astype(jnp.float32)
        for j in range(128, width, 128):
            total += staged[r, j:j + 128].astype(jnp.float32)
        sums[pl.ds(k, 1), :] = jnp.sum(total.T, axis=0, keepdims=True)
        return carry

    def standardize_rows(k, carry):
        r = pl.ds(pl.multiple_of(k * 128, 128), 128)
        share = GENES / jnp.broadcast_to(sums[pl.ds(k, 1), :], (128, 128)).T
        for j in range(0, width, 128):
            lognorm = jnp.log1p(staged[r, j:j + 128].astype(jnp.float32) * share)
            xs[zi, gi, r, j:j + 128] = (
                (lognorm - mean_ref[:, j:j + 128]) / scale_ref[:, j:j + 128]
            ).astype(jnp.bfloat16)
        return carry

    sums[...] = jnp.zeros_like(sums)
    for h in range(2):
        loads[h].wait()
        lax.fori_loop(cuts[h] // 128, cuts[h + 1] // 128, add_up, 0)
    ends_of_line = (zi == 0).astype(jnp.int32) + (zi == last).astype(jnp.int32)
    pl.semaphore_wait(barrier, len(peers) + 2 - ends_of_line)
    tells = [
        pltpu.make_async_remote_copy(
            src_ref=sums, dst_ref=heard.at[i], send_sem=sums_send.at[i], recv_sem=sums_recv.at[i],
            device_id=peer, device_id_type=MESH,
        )
        for i, peer in enumerate(peers)
    ]
    for dma in tells:
        dma.start()
    for dma in tells:
        dma.wait()
    whole = sums[...]
    for i in range(len(peers)):
        whole += heard[i]
    sums[...] = whole
    for h in range(2):
        lax.fori_loop(cuts[h] // 128, cuts[h + 1] // 128, standardize_rows, 0)
        sends(zi, True, h, start)
    acc[...] = jnp.zeros_like(acc)

    def deliver(a):
        acc[a] = acc[a] * (1.0 / (nz * cuts[2]))
        pltpu.make_async_copy(acc.at[a], out_ref.at[:, a, :], out_sem.at[a]).start()

    def step(d, carry):
        @pl.when(d == nz)
        def _():
            deliver(gi)
            deliver(g_sib)

        pl.when((d > 0) & (d < nz))(lambda: forward(d))
        ends(d)
        pl.when(d < nz)(lambda: near(d))
        pl.when(d > 0)(lambda: far(d - 1))
        return carry

    lax.fori_loop(0, nz + 1, step, 0)
    deliver(g_across)
    deliver((1 - x) * 2 + (1 - c))

    def drain(z, carry):
        for h in range(2):
            for mine in (True, False):
                sends(z, mine, h, finish)
        return carry

    lax.fori_loop(0, nz, drain, 0)
    for a in range(acc.shape[0]):
        pltpu.make_async_copy(acc.at[a], out_ref.at[:, a, :], out_sem.at[a]).wait()


def copy_kernel(src, dst, sems):
    n = sems.shape[0]
    each = src.shape[0] // n
    dmas = [
        pltpu.make_async_copy(
            src.at[pl.ds(i * each, each)], dst.at[pl.ds(i * each, each)], sems.at[i]
        )
        for i in range(n)
    ]
    for dma in dmas:
        dma.start()
    for dma in dmas:
        dma.wait()


def line_plan(counts, gene_mean, gene_scale):
    nz, n_grow = lax.axis_size("cells"), lax.axis_size("grow")
    cell_rows, width = counts.shape[0], counts.shape[3]
    rows = 2 * width // nz
    cuts = (0, -(-cell_rows // 256) * 128, cell_rows)
    flops = 2 * rows * n_grow * width * nz * cell_rows
    scaled = pl.pallas_call(
        functools.partial(gram_kernel, nz, rows, cuts),
        out_shape=jax.ShapeDtypeStruct((rows, n_grow, width), jnp.float32),
        in_specs=[
            pl.BlockSpec(memory_space=pl.ANY),
            pl.BlockSpec(memory_space=pltpu.VMEM),
            pl.BlockSpec(memory_space=pltpu.VMEM),
        ],
        out_specs=pl.BlockSpec(memory_space=pl.ANY),
        scratch_shapes=[
            pltpu.VMEM((cell_rows, width), jnp.int32),
            pltpu.VMEM((-(-cell_rows // 1024) * 8, 128), jnp.float32),
            pltpu.VMEM((7, -(-cell_rows // 1024) * 8, 128), jnp.float32),
            pltpu.VMEM((nz, n_grow, cell_rows, width), jnp.bfloat16),
            pltpu.VMEM((nz, cell_rows, rows), jnp.bfloat16),
            pltpu.VMEM((nz, rows, cell_rows), jnp.bfloat16),
            pltpu.VMEM((n_grow, rows, width), jnp.float32),
            pltpu.SemaphoreType.DMA((2,)),
            pltpu.SemaphoreType.DMA((7,)),
            pltpu.SemaphoreType.DMA((7,)),
            pltpu.SemaphoreType.DMA((nz, n_grow, 2)),
            pltpu.SemaphoreType.DMA((4, nz, 2, 2)),
            pltpu.SemaphoreType.DMA((nz, 2)),
            pltpu.SemaphoreType.DMA((nz, 2)),
            pltpu.SemaphoreType.DMA((n_grow,)),
        ],
        compiler_params=pltpu.CompilerParams(
            collective_id=0, has_side_effects=True, vmem_limit_bytes=62 * 2**20
        ),
        cost_estimate=pl.CostEstimate(
            flops=flops, bytes_accessed=4 * rows * n_grow * width, transcendentals=0
        ),
    )(counts.reshape(cell_rows, 1, width), gene_mean.reshape(1, width), gene_scale.reshape(1, width))
    copied = pl.pallas_call(
        copy_kernel,
        out_shape=jax.ShapeDtypeStruct(scaled.shape, scaled.dtype),
        in_specs=[pl.BlockSpec(memory_space=pl.ANY)],
        out_specs=pl.BlockSpec(memory_space=pl.ANY),
        scratch_shapes=[pltpu.SemaphoreType.DMA((8,))],
    )(scaled)
    return copied.reshape(1, rows, 1, n_grow, width)


def sum_plan(counts, gene_mean, gene_scale):
    cell_rows, width = counts.shape[0], counts.shape[3]
    standard = standardize(counts, gene_mean, gene_scale).reshape(cell_rows, 1, width)
    n_grow, n_gcol, n_cells = (lax.axis_size(a) for a in ("grow", "gcol", "cells"))
    row_flat = lax.all_gather(standard, "gcol", axis=1, tiled=True).reshape(cell_rows, -1)
    col_flat = lax.all_gather(standard, "grow", axis=1, tiled=True).reshape(cell_rows, -1)
    owned = row_flat.shape[1] // n_cells
    summed = lax.psum_scatter(
        lax.dot_general(
            row_flat, col_flat, (((0,), (0,)), ((), ())), preferred_element_type=jnp.float32
        ),
        "cells",
        scatter_dimension=0,
        tiled=True,
    )
    return (summed / (n_cells * cell_rows)).reshape(1, owned, 1, n_grow, width)


def solution(mesh):
    placed = (P("cells", "grow", "gcol", None), P("grow", "gcol", None), P("grow", "gcol", None))
    sizes = tuple(mesh.shape[a] for a in ("cells", "grow", "gcol"))
    return jax.shard_map(
        line_plan if sizes == (4, 4, 2) else sum_plan,
        mesh=mesh,
        in_specs=placed,
        out_specs=P("grow", "cells", "gcol", None, None),
        check_vma=False,
    )
```

```python
import functools

import jax
import jax.numpy as jnp
from jax import lax
from jax.experimental import pallas as pl
from jax.experimental.pallas import tpu as pltpu
from jax.sharding import PartitionSpec as P

GENES = 8192
MESH = pl.DeviceIdType.MESH
SIB, UP, DOWN, ACROSS = range(4)
TILE = 256


def standardize(counts, gene_mean, gene_scale):
    cell_rows, width = counts.shape[0], counts.shape[3]
    local = counts.reshape(cell_rows, width).astype(jnp.float32)
    totals = lax.psum(jnp.sum(local, axis=1), ("grow", "gcol"))
    lognorm = jnp.log1p(local * GENES / totals[:, None])
    return ((lognorm - gene_mean.reshape(1, width)) / gene_scale.reshape(1, width)).astype(
        jnp.bfloat16
    )


def gram_kernel(nz, rows, cuts, counts_ref, mean_ref, scale_ref, out_ref,
                staged, sums, heard, xs, landed, turned, acc,
                load_sem, sums_recv, sums_send, recv_sem, send_sem, rows_recv, rows_send, out_sem):
    zi, gi, yi = lax.axis_index("cells"), lax.axis_index("grow"), lax.axis_index("gcol")
    width = xs.shape[3]
    last = nz - 1
    x, c = gi // 2, gi % 2
    g_sib = x * 2 + (1 - c)
    g_across = (1 - x) * 2 + c
    target = {
        SIB: {"grow": g_sib},
        UP: {"cells": jnp.minimum(zi + 1, last)},
        DOWN: {"cells": jnp.maximum(zi - 1, 0)},
        ACROSS: {"grow": g_across},
    }
    owner = (zi * 2) // nz == yi
    own_col = pl.multiple_of((zi % (nz // 2)) * rows, rows)

    barrier = pltpu.get_barrier_semaphore()

    def greet(to):
        pl.semaphore_signal(barrier, inc=1, device_id=to, device_id_type=MESH)

    peers = [
        {"grow": (gi + dg) % 4, "gcol": (yi + dy) % 2}
        for dg in range(4) for dy in range(2) if dg or dy
    ]
    for peer in peers:
        greet(peer)
    pl.when(zi < last)(lambda: greet(target[UP]))
    pl.when(zi > 0)(lambda: greet(target[DOWN]))
    loads = [
        pltpu.make_async_copy(
            counts_ref.at[pl.ds(cuts[h], cuts[h + 1] - cuts[h]), 0, :],
            staged.at[pl.ds(cuts[h], cuts[h + 1] - cuts[h]), :], load_sem.at[h],
        )
        for h in range(2)
    ]
    for dma in loads:
        dma.start()

    def part(h):
        return pl.ds(cuts[h], cuts[h + 1] - cuts[h])

    def copy(kind, z, g, h):
        ref = xs.at[z, g, part(h), :]
        return pltpu.make_async_remote_copy(
            src_ref=ref, dst_ref=ref,
            send_sem=send_sem.at[kind, z, g // 2, h], recv_sem=recv_sem.at[z, g, h],
            device_id=target[kind], device_id_type=MESH,
        )

    def rows_copy(z, h):
        return pltpu.make_async_remote_copy(
            src_ref=xs.at[z, gi, part(h), pl.ds(own_col, rows)], dst_ref=landed.at[z, part(h), :],
            send_sem=rows_send.at[z, h], recv_sem=rows_recv.at[z, h],
            device_id={"gcol": 1 - yi}, device_id_type=MESH,
        )

    def sends(z, mine, h, act):
        g = gi if mine else g_across
        if mine:
            pl.when((z <= zi) & (zi < last))(lambda: act(copy(UP, z, g, h)))
            pl.when((z >= zi) & (zi > 0))(lambda: act(copy(DOWN, z, g, h)))
            if h == 0:
                act(copy(ACROSS, z, g, h))
            else:
                by_line = ((z == 0) & (zi != 0)) | ((z == last) & (zi != last))
                pl.when(jnp.logical_not(by_line))(lambda: act(copy(ACROSS, z, g, h)))
            pl.when(owner)(lambda: act(rows_copy(z, h)))
        elif h == 1:
            pl.when((z == 0) & (zi < last))(lambda: act(copy(UP, z, g, h)))
            pl.when((z == last) & (zi > 0))(lambda: act(copy(DOWN, z, g, h)))
        act(copy(SIB, z, g, h))

    def start(dma):
        dma.start()

    def finish(dma):
        dma.wait_send()

    def arrive(z, g, h):
        copy(SIB, z, g, h).wait_recv()

    def place(d, side):
        z = zi - d + 2 * d * side
        valid = (z >= 0) & (z <= last) & ((d > 0) | (side == 0))
        return z, valid

    def forward(d):
        for h in range(2):
            for side in range(2):
                z, valid = place(d, side)

                @pl.when(valid)
                def _():
                    pl.when(d > 0)(lambda: arrive(z, gi, h))
                    sends(z, True, h, start)

    def ends(d):
        for z, hit in ((0, zi == d - 1), (last, last - zi == d - 1)):
            @pl.when(hit)
            def _():
                arrive(z, g_across, 1)
                sends(z, False, 1, start)

    def turn(z, h):
        for k in range(cuts[h], cuts[h + 1], 128):
            @pl.when(owner)
            def _():
                turned[z, :, k:k + 128] = xs[z, gi, k:k + 128, pl.ds(own_col, rows)].T

            @pl.when(jnp.logical_not(owner))
            def _():
                turned[z, :, k:k + 128] = landed[z, k:k + 128, :].T

    def multiply(z, g, h):
        tiles = width // TILE

        def body(i, carry):
            a = (g // 2) * 2 + i // tiles
            n = pl.ds(pl.multiple_of((i % tiles) * TILE, TILE), TILE)
            acc[a, :, n] += jnp.dot(
                turned[z, :, part(h)], xs[z, a, part(h), n], preferred_element_type=jnp.float32
            )
            return carry

        lax.fori_loop(0, 2 * tiles, body, 0)

    def near(d):
        def body(side, carry):
            z, valid = place(d, side)

            @pl.when(valid)
            def _():
                for h in range(2):
                    pl.when(jnp.logical_not(owner))(lambda: rows_copy(z, h).wait_recv())
                    turn(z, h)
                    arrive(z, g_sib, h)
                    multiply(z, gi, h)
            return carry

        lax.fori_loop(0, 2, body, 0)

    def far(d):
        def body(side, carry):
            z, valid = place(d, side)

            def take(h):
                arrive(z, g_across, h)
                start(copy(SIB, z, g_across, h))

            def use(h):
                arrive(z, (1 - x) * 2 + (1 - c), h)
                multiply(z, g_across, h)

            at_end = (z == 0) | (z == last)

            @pl.when(valid)
            def _():
                pl.when(at_end)(lambda: use(1))
                take(0)
                use(0)

                @pl.when(jnp.logical_not(at_end))
                def _():
                    take(1)
                    use(1)
            return carry

        lax.fori_loop(0, 2, body, 0)

    def add_up(k, carry):
        r = pl.ds(pl.multiple_of(k * 128, 128), 128)
        total = staged[r, 0:128].astype(jnp.float32)
        for j in range(128, width, 128):
            total += staged[r, j:j + 128].astype(jnp.float32)
        sums[pl.ds(k, 1), :] = jnp.sum(total.T, axis=0, keepdims=True)
        return carry

    def standardize_rows(k, carry):
        r = pl.ds(pl.multiple_of(k * 128, 128), 128)
        share = GENES / jnp.broadcast_to(sums[pl.ds(k, 1), :], (128, 128)).T
        for j in range(0, width, 128):
            lognorm = jnp.log1p(staged[r, j:j + 128].astype(jnp.float32) * share)
            xs[zi, gi, r, j:j + 128] = (
                (lognorm - mean_ref[:, j:j + 128]) / scale_ref[:, j:j + 128]
            ).astype(jnp.bfloat16)
        return carry

    sums[...] = jnp.zeros_like(sums)
    for h in range(2):
        loads[h].wait()
        lax.fori_loop(cuts[h] // 128, cuts[h + 1] // 128, add_up, 0)
    ends_of_line = (zi == 0).astype(jnp.int32) + (zi == last).astype(jnp.int32)
    pl.semaphore_wait(barrier, len(peers) + 2 - ends_of_line)
    tells = [
        pltpu.make_async_remote_copy(
            src_ref=sums, dst_ref=heard.at[i], send_sem=sums_send.at[i], recv_sem=sums_recv.at[i],
            device_id=peer, device_id_type=MESH,
        )
        for i, peer in enumerate(peers)
    ]
    for dma in tells:
        dma.start()
    for dma in tells:
        dma.wait()
    whole = sums[...]
    for i in range(len(peers)):
        whole += heard[i]
    sums[...] = whole
    for h in range(2):
        lax.fori_loop(cuts[h] // 128, cuts[h + 1] // 128, standardize_rows, 0)
        sends(zi, True, h, start)
    acc[...] = jnp.zeros_like(acc)

    def deliver(a):
        acc[a] = acc[a] * (1.0 / (nz * cuts[2]))
        pltpu.make_async_copy(acc.at[a], out_ref.at[:, a, :], out_sem.at[a]).start()

    def step(d, carry):
        @pl.when(d == nz)
        def _():
            deliver(gi)
            deliver(g_sib)

        pl.when((d > 0) & (d < nz))(lambda: forward(d))
        ends(d)
        pl.when(d < nz)(lambda: near(d))
        pl.when(d > 0)(lambda: far(d - 1))
        return carry

    lax.fori_loop(0, nz + 1, step, 0)
    deliver(g_across)
    deliver((1 - x) * 2 + (1 - c))

    def drain(z, carry):
        for h in range(2):
            for mine in (True, False):
                sends(z, mine, h, finish)
        return carry

    lax.fori_loop(0, nz, drain, 0)
    for a in range(acc.shape[0]):
        pltpu.make_async_copy(acc.at[a], out_ref.at[:, a, :], out_sem.at[a]).wait()


def copy_kernel(src, dst, held, load_sems, store_sems):
    n = load_sems.shape[0]
    each = src.shape[0] // n
    at = [pl.ds(i * each, each) for i in range(n)]
    loads = [pltpu.make_async_copy(src.at[r], held.at[r], load_sems.at[i]) for i, r in enumerate(at)]
    stores = [pltpu.make_async_copy(held.at[r], dst.at[r], store_sems.at[i]) for i, r in enumerate(at)]
    for dma in loads:
        dma.start()
    for load, store in zip(loads, stores):
        load.wait()
        store.start()
    for dma in stores:
        dma.wait()


def line_plan(counts, gene_mean, gene_scale):
    nz, n_grow = lax.axis_size("cells"), lax.axis_size("grow")
    cell_rows, width = counts.shape[0], counts.shape[3]
    rows = 2 * width // nz
    cuts = (0, cell_rows // 256 * 128, cell_rows)
    flops = 2 * rows * n_grow * width * nz * cell_rows
    scaled = pl.pallas_call(
        functools.partial(gram_kernel, nz, rows, cuts),
        out_shape=jax.ShapeDtypeStruct((rows, n_grow, width), jnp.float32),
        in_specs=[
            pl.BlockSpec(memory_space=pl.ANY),
            pl.BlockSpec(memory_space=pltpu.VMEM),
            pl.BlockSpec(memory_space=pltpu.VMEM),
        ],
        out_specs=pl.BlockSpec(memory_space=pl.ANY),
        scratch_shapes=[
            pltpu.VMEM((cell_rows, width), jnp.int32),
            pltpu.VMEM((-(-cell_rows // 1024) * 8, 128), jnp.float32),
            pltpu.VMEM((7, -(-cell_rows // 1024) * 8, 128), jnp.float32),
            pltpu.VMEM((nz, n_grow, cell_rows, width), jnp.bfloat16),
            pltpu.VMEM((nz, cell_rows, rows), jnp.bfloat16),
            pltpu.VMEM((nz, rows, cell_rows), jnp.bfloat16),
            pltpu.VMEM((n_grow, rows, width), jnp.float32),
            pltpu.SemaphoreType.DMA((2,)),
            pltpu.SemaphoreType.DMA((7,)),
            pltpu.SemaphoreType.DMA((7,)),
            pltpu.SemaphoreType.DMA((nz, n_grow, 2)),
            pltpu.SemaphoreType.DMA((4, nz, 2, 2)),
            pltpu.SemaphoreType.DMA((nz, 2)),
            pltpu.SemaphoreType.DMA((nz, 2)),
            pltpu.SemaphoreType.DMA((n_grow,)),
        ],
        compiler_params=pltpu.CompilerParams(
            collective_id=0, has_side_effects=True, vmem_limit_bytes=62 * 2**20
        ),
        cost_estimate=pl.CostEstimate(
            flops=flops, bytes_accessed=4 * rows * n_grow * width, transcendentals=0
        ),
    )(counts.reshape(cell_rows, 1, width), gene_mean.reshape(1, width), gene_scale.reshape(1, width))
    copied = pl.pallas_call(
        copy_kernel,
        out_shape=jax.ShapeDtypeStruct(scaled.shape, scaled.dtype),
        in_specs=[pl.BlockSpec(memory_space=pl.ANY)],
        out_specs=pl.BlockSpec(memory_space=pl.ANY),
        scratch_shapes=[
            pltpu.VMEM(scaled.shape, scaled.dtype),
            pltpu.SemaphoreType.DMA((16,)),
            pltpu.SemaphoreType.DMA((16,)),
        ],
        compiler_params=pltpu.CompilerParams(vmem_limit_bytes=62 * 2**20),
    )(scaled)
    return copied.reshape(1, rows, 1, n_grow, width)


def sum_plan(counts, gene_mean, gene_scale):
    cell_rows, width = counts.shape[0], counts.shape[3]
    standard = standardize(counts, gene_mean, gene_scale).reshape(cell_rows, 1, width)
    n_grow, n_gcol, n_cells = (lax.axis_size(a) for a in ("grow", "gcol", "cells"))
    row_flat = lax.all_gather(standard, "gcol", axis=1, tiled=True).reshape(cell_rows, -1)
    col_flat = lax.all_gather(standard, "grow", axis=1, tiled=True).reshape(cell_rows, -1)
    owned = row_flat.shape[1] // n_cells
    summed = lax.psum_scatter(
        lax.dot_general(
            row_flat, col_flat, (((0,), (0,)), ((), ())), preferred_element_type=jnp.float32
        ),
        "cells",
        scatter_dimension=0,
        tiled=True,
    )
    return (summed / (n_cells * cell_rows)).reshape(1, owned, 1, n_grow, width)


def solution(mesh):
    placed = (P("cells", "grow", "gcol", None), P("grow", "gcol", None), P("grow", "gcol", None))
    sizes = tuple(mesh.shape[a] for a in ("cells", "grow", "gcol"))
    return jax.shard_map(
        line_plan if sizes == (4, 4, 2) else sum_plan,
        mesh=mesh,
        in_specs=placed,
        out_specs=P("grow", "cells", "gcol", None, None),
        check_vma=False,
    )
```

```python
import functools

import jax
import jax.numpy as jnp
from jax import lax
from jax.experimental import pallas as pl
from jax.experimental.pallas import tpu as pltpu
from jax.sharding import PartitionSpec as P

GENES = 8192
MESH = pl.DeviceIdType.MESH
SIB, UP, DOWN, ACROSS = range(4)
TILE = 256


def standardize(counts, gene_mean, gene_scale):
    cell_rows, width = counts.shape[0], counts.shape[3]
    local = counts.reshape(cell_rows, width).astype(jnp.float32)
    totals = lax.psum(jnp.sum(local, axis=1), ("grow", "gcol"))
    lognorm = jnp.log1p(local * GENES / totals[:, None])
    return ((lognorm - gene_mean.reshape(1, width)) / gene_scale.reshape(1, width)).astype(
        jnp.bfloat16
    )


def gram_kernel(nz, rows, cuts, m, counts_ref, mean_ref, scale_ref, out_ref,
                staged, sums, heard, xs, landed, turned, acc,
                load_sem, sums_recv, sums_send, recv_sem, send_sem, rows_recv, rows_send, out_sem):
    zi, gi, yi = lax.axis_index("cells"), lax.axis_index("grow"), lax.axis_index("gcol")
    width = xs.shape[3]
    last = nz - 1
    parts = len(cuts) - 1
    x, c = gi // 2, gi % 2
    g_sib = x * 2 + (1 - c)
    g_across = (1 - x) * 2 + c
    g_other = (1 - x) * 2 + (1 - c)
    target = {
        SIB: {"grow": g_sib},
        UP: {"cells": jnp.minimum(zi + 1, last)},
        DOWN: {"cells": jnp.maximum(zi - 1, 0)},
        ACROSS: {"grow": g_across},
    }
    owner = (zi * 2) // nz == yi
    own_col = pl.multiple_of((zi % (nz // 2)) * rows, rows)

    barrier = pltpu.get_barrier_semaphore()

    def greet(to):
        pl.semaphore_signal(barrier, inc=1, device_id=to, device_id_type=MESH)

    peers = [
        {"grow": (gi + dg) % 4, "gcol": (yi + dy) % 2}
        for dg in range(4) for dy in range(2) if dg or dy
    ]
    for peer in peers:
        greet(peer)
    pl.when(zi < last)(lambda: greet(target[UP]))
    pl.when(zi > 0)(lambda: greet(target[DOWN]))
    loads = [
        pltpu.make_async_copy(
            counts_ref.at[pl.ds(cuts[h], cuts[h + 1] - cuts[h]), 0, :],
            staged.at[pl.ds(cuts[h], cuts[h + 1] - cuts[h]), :], load_sem.at[h],
        )
        for h in range(parts)
    ]
    for dma in loads:
        dma.start()

    def part(h):
        return pl.ds(cuts[h], cuts[h + 1] - cuts[h])

    def copy(kind, z, g, h):
        ref = xs.at[z, g, part(h), :]
        return pltpu.make_async_remote_copy(
            src_ref=ref, dst_ref=ref,
            send_sem=send_sem.at[kind, z, g // 2, h], recv_sem=recv_sem.at[z, g, h],
            device_id=target[kind], device_id_type=MESH,
        )

    def rows_copy(z, h):
        return pltpu.make_async_remote_copy(
            src_ref=xs.at[z, gi, part(h), pl.ds(own_col, rows)], dst_ref=landed.at[z, part(h), :],
            send_sem=rows_send.at[z, h], recv_sem=rows_recv.at[z, h],
            device_id={"gcol": 1 - yi}, device_id_type=MESH,
        )

    def sends(z, mine, h, act):
        g = gi if mine else g_across
        if mine:
            pl.when((z <= zi) & (zi < last))(lambda: act(copy(UP, z, g, h)))
            pl.when((z >= zi) & (zi > 0))(lambda: act(copy(DOWN, z, g, h)))
            if h < m:
                act(copy(ACROSS, z, g, h))
            else:
                by_line = ((z == 0) & (zi != 0)) | ((z == last) & (zi != last))
                pl.when(jnp.logical_not(by_line))(lambda: act(copy(ACROSS, z, g, h)))
            pl.when(owner)(lambda: act(rows_copy(z, h)))
        elif h >= m:
            pl.when((z == 0) & (zi < last))(lambda: act(copy(UP, z, g, h)))
            pl.when((z == last) & (zi > 0))(lambda: act(copy(DOWN, z, g, h)))
        act(copy(SIB, z, g, h))

    def start(dma):
        dma.start()

    def finish(dma):
        dma.wait_send()

    def arrive(z, g, h):
        copy(SIB, z, g, h).wait_recv()

    def place(d, side):
        z = zi - d + 2 * d * side
        valid = (z >= 0) & (z <= last) & ((d > 0) | (side == 0))
        return z, valid

    def forward(d):
        for h in range(parts):
            for side in range(2):
                z, valid = place(d, side)

                @pl.when(valid)
                def _():
                    pl.when(d > 0)(lambda: arrive(z, gi, h))
                    sends(z, True, h, start)

    def ends(d):
        for z, hit in ((0, zi == d - 1), (last, last - zi == d - 1)):
            @pl.when(hit)
            def _():
                for h in range(m, parts):
                    arrive(z, g_across, h)
                    sends(z, False, h, start)

    def turn(z):
        for k in range(0, cuts[-1], 128):
            @pl.when(owner)
            def _():
                turned[z, :, k:k + 128] = xs[z, gi, k:k + 128, pl.ds(own_col, rows)].T

            @pl.when(jnp.logical_not(owner))
            def _():
                turned[z, :, k:k + 128] = landed[z, k:k + 128, :].T

    def multiply(z, a, lo, hi):
        def body(i, carry):
            n = pl.ds(pl.multiple_of(i * TILE, TILE), TILE)
            acc[a, :, n] += jnp.dot(
                turned[z, :, lo:hi], xs[z, a, lo:hi, n], preferred_element_type=jnp.float32
            )
            return carry

        lax.fori_loop(0, width // TILE, body, 0)

    def near(d):
        def body(side, carry):
            z, valid = place(d, side)

            @pl.when(valid)
            def _():
                @pl.when(jnp.logical_not(owner))
                def _():
                    for h in range(parts):
                        rows_copy(z, h).wait_recv()

                turn(z)
                multiply(z, gi, 0, cuts[-1])
                for h in range(parts):
                    arrive(z, g_sib, h)
                multiply(z, g_sib, 0, cuts[-1])
            return carry

        lax.fori_loop(0, 2, body, 0)

    def deliver(a):
        acc[a] = acc[a] * (1.0 / (nz * cuts[-1]))
        pltpu.make_async_copy(acc.at[a], out_ref.at[:, a, :], out_sem.at[a]).start()

    def far(d):
        def body(side, carry):
            z, valid = place(d, side)
            at_end = (z == 0) | (z == last)

            def take(h):
                arrive(z, g_across, h)
                start(copy(SIB, z, g_across, h))

            @pl.when(valid & jnp.logical_not(at_end))
            def _():
                for h in range(parts):
                    take(h)
                multiply(z, g_across, 0, cuts[-1])
                for h in range(parts):
                    arrive(z, g_other, h)
                multiply(z, g_other, 0, cuts[-1])

            @pl.when(valid & at_end)
            def _():
                order = sorted(range(parts), key=lambda h: (h - m + 0.5 if h >= m else h))
                for h in order:
                    if h < m:
                        take(h)
                    else:
                        pl.when(d == last)(lambda: take(h))
                    multiply(z, g_across, cuts[h], cuts[h + 1])
                    if h == order[-1]:
                        pl.when(d == last)(lambda: deliver(g_across))
                    arrive(z, g_other, h)
                    multiply(z, g_other, cuts[h], cuts[h + 1])
            return carry

        lax.fori_loop(0, 2, body, 0)

    def add_up(k, carry):
        r = pl.ds(pl.multiple_of(k * 128, 128), 128)
        total = staged[r, 0:128].astype(jnp.float32)
        for j in range(128, width, 128):
            total += staged[r, j:j + 128].astype(jnp.float32)
        sums[pl.ds(k, 1), :] = jnp.sum(total.T, axis=0, keepdims=True)
        return carry

    def standardize_rows(k, carry):
        r = pl.ds(pl.multiple_of(k * 128, 128), 128)
        share = GENES / jnp.broadcast_to(sums[pl.ds(k, 1), :], (128, 128)).T
        for j in range(0, width, 128):
            lognorm = jnp.log1p(staged[r, j:j + 128].astype(jnp.float32) * share)
            xs[zi, gi, r, j:j + 128] = (
                (lognorm - mean_ref[:, j:j + 128]) / scale_ref[:, j:j + 128]
            ).astype(jnp.bfloat16)
        return carry

    sums[...] = jnp.zeros_like(sums)
    for h in range(parts):
        loads[h].wait()
        lax.fori_loop(cuts[h] // 128, cuts[h + 1] // 128, add_up, 0)
    ends_of_line = (zi == 0).astype(jnp.int32) + (zi == last).astype(jnp.int32)
    pl.semaphore_wait(barrier, len(peers) + 2 - ends_of_line)
    tells = [
        pltpu.make_async_remote_copy(
            src_ref=sums, dst_ref=heard.at[i], send_sem=sums_send.at[i], recv_sem=sums_recv.at[i],
            device_id=peer, device_id_type=MESH,
        )
        for i, peer in enumerate(peers)
    ]
    for dma in tells:
        dma.start()
    for dma in tells:
        dma.wait()
    whole = sums[...]
    for i in range(len(peers)):
        whole += heard[i]
    sums[...] = whole
    for h in range(parts):
        lax.fori_loop(cuts[h] // 128, cuts[h + 1] // 128, standardize_rows, 0)
        sends(zi, True, h, start)
    acc[...] = jnp.zeros_like(acc)

    def step(d, carry):
        @pl.when(d == nz)
        def _():
            deliver(gi)
            deliver(g_sib)

        pl.when((d > 0) & (d < nz))(lambda: forward(d))
        pl.when(d < nz)(lambda: ends(d))
        pl.when(d < nz)(lambda: near(d))
        pl.when(d > 0)(lambda: far(d - 1))
        return carry

    lax.fori_loop(0, nz + 1, step, 0)
    pl.when((zi > 0) & (zi < last))(lambda: deliver(g_across))
    deliver(g_other)

    def drain(z, carry):
        for h in range(parts):
            for mine in (True, False):
                sends(z, mine, h, finish)
        return carry

    lax.fori_loop(0, nz, drain, 0)
    for a in range(acc.shape[0]):
        pltpu.make_async_copy(acc.at[a], out_ref.at[:, a, :], out_sem.at[a]).wait()


def copy_kernel(src, dst, held, load_sems, store_sems):
    n = load_sems.shape[0]
    each = src.shape[0] // n
    at = [pl.ds(i * each, each) for i in range(n)]
    loads = [pltpu.make_async_copy(src.at[r], held.at[r], load_sems.at[i]) for i, r in enumerate(at)]
    stores = [pltpu.make_async_copy(held.at[r], dst.at[r], store_sems.at[i]) for i, r in enumerate(at)]
    for dma in loads:
        dma.start()
    for load, store in zip(loads, stores):
        load.wait()
        store.start()
    for dma in stores:
        dma.wait()


def line_plan(counts, gene_mean, gene_scale):
    nz, n_grow = lax.axis_size("cells"), lax.axis_size("grow")
    cell_rows, width = counts.shape[0], counts.shape[3]
    rows = 2 * width // nz
    cuts, m = (0, 256, 512, 640, 896, cell_rows), 3
    flops = 2 * rows * n_grow * width * nz * cell_rows
    scaled = pl.pallas_call(
        functools.partial(gram_kernel, nz, rows, cuts, m),
        out_shape=jax.ShapeDtypeStruct((rows, n_grow, width), jnp.float32),
        in_specs=[
            pl.BlockSpec(memory_space=pl.ANY),
            pl.BlockSpec(memory_space=pltpu.VMEM),
            pl.BlockSpec(memory_space=pltpu.VMEM),
        ],
        out_specs=pl.BlockSpec(memory_space=pl.ANY),
        scratch_shapes=[
            pltpu.VMEM((cell_rows, width), jnp.int32),
            pltpu.VMEM((-(-cell_rows // 1024) * 8, 128), jnp.float32),
            pltpu.VMEM((7, -(-cell_rows // 1024) * 8, 128), jnp.float32),
            pltpu.VMEM((nz, n_grow, cell_rows, width), jnp.bfloat16),
            pltpu.VMEM((nz, cell_rows, rows), jnp.bfloat16),
            pltpu.VMEM((nz, rows, cell_rows), jnp.bfloat16),
            pltpu.VMEM((n_grow, rows, width), jnp.float32),
            pltpu.SemaphoreType.DMA((len(cuts) - 1,)),
            pltpu.SemaphoreType.DMA((7,)),
            pltpu.SemaphoreType.DMA((7,)),
            pltpu.SemaphoreType.DMA((nz, n_grow, len(cuts) - 1)),
            pltpu.SemaphoreType.DMA((4, nz, 2, len(cuts) - 1)),
            pltpu.SemaphoreType.DMA((nz, len(cuts) - 1)),
            pltpu.SemaphoreType.DMA((nz, len(cuts) - 1)),
            pltpu.SemaphoreType.DMA((n_grow,)),
        ],
        compiler_params=pltpu.CompilerParams(
            collective_id=0, has_side_effects=True, vmem_limit_bytes=62 * 2**20
        ),
        cost_estimate=pl.CostEstimate(
            flops=flops, bytes_accessed=4 * rows * n_grow * width, transcendentals=0
        ),
    )(counts.reshape(cell_rows, 1, width), gene_mean.reshape(1, width), gene_scale.reshape(1, width))
    copied = pl.pallas_call(
        copy_kernel,
        out_shape=jax.ShapeDtypeStruct(scaled.shape, scaled.dtype),
        in_specs=[pl.BlockSpec(memory_space=pl.ANY)],
        out_specs=pl.BlockSpec(memory_space=pl.ANY),
        scratch_shapes=[
            pltpu.VMEM(scaled.shape, scaled.dtype),
            pltpu.SemaphoreType.DMA((16,)),
            pltpu.SemaphoreType.DMA((16,)),
        ],
        compiler_params=pltpu.CompilerParams(vmem_limit_bytes=62 * 2**20),
    )(scaled)
    return copied.reshape(1, rows, 1, n_grow, width)


def sum_plan(counts, gene_mean, gene_scale):
    cell_rows, width = counts.shape[0], counts.shape[3]
    standard = standardize(counts, gene_mean, gene_scale).reshape(cell_rows, 1, width)
    n_grow, n_gcol, n_cells = (lax.axis_size(a) for a in ("grow", "gcol", "cells"))
    row_flat = lax.all_gather(standard, "gcol", axis=1, tiled=True).reshape(cell_rows, -1)
    col_flat = lax.all_gather(standard, "grow", axis=1, tiled=True).reshape(cell_rows, -1)
    owned = row_flat.shape[1] // n_cells
    summed = lax.psum_scatter(
        lax.dot_general(
            row_flat, col_flat, (((0,), (0,)), ((), ())), preferred_element_type=jnp.float32
        ),
        "cells",
        scatter_dimension=0,
        tiled=True,
    )
    return (summed / (n_cells * cell_rows)).reshape(1, owned, 1, n_grow, width)


def solution(mesh):
    placed = (P("cells", "grow", "gcol", None), P("grow", "gcol", None), P("grow", "gcol", None))
    sizes = tuple(mesh.shape[a] for a in ("cells", "grow", "gcol"))
    return jax.shard_map(
        line_plan if sizes == (4, 4, 2) else sum_plan,
        mesh=mesh,
        in_specs=placed,
        out_specs=P("grow", "cells", "gcol", None, None),
        check_vma=False,
    )
```

```python
import functools

import jax
import jax.numpy as jnp
from jax import lax
from jax.experimental import pallas as pl
from jax.experimental.pallas import tpu as pltpu
from jax.sharding import PartitionSpec as P

GENES = 8192
MESH = pl.DeviceIdType.MESH
SIB, UP, DOWN, ACROSS = range(4)
TILE = 256
LEVELS = 32767.0


def standardize(counts, gene_mean, gene_scale):
    cell_rows, width = counts.shape[0], counts.shape[3]
    local = counts.reshape(cell_rows, width).astype(jnp.float32)
    totals = lax.psum(jnp.sum(local, axis=1), ("grow", "gcol"))
    lognorm = jnp.log1p(local * GENES / totals[:, None])
    return ((lognorm - gene_mean.reshape(1, width)) / gene_scale.reshape(1, width)).astype(
        jnp.bfloat16
    )


def gram_kernel(nz, rows, cuts, m, counts_ref, mean_ref, scale_ref, out_ref,
                staged, sums, heard, xs, landed, turned, acc, told, asked, told_unit, asked_unit,
                load_sem, sums_recv, sums_send, recv_sem, send_sem, rows_recv, rows_send, out_sem,
                more_recv, more_send, asked_sem, told_sem):
    zi, gi, yi = lax.axis_index("cells"), lax.axis_index("grow"), lax.axis_index("gcol")
    width = xs.shape[3]
    last = nz - 1
    parts = len(cuts) - 1
    x, c = gi // 2, gi % 2
    g_sib = x * 2 + (1 - c)
    g_across = (1 - x) * 2 + c
    g_other = (1 - x) * 2 + (1 - c)
    target = {
        SIB: {"grow": g_sib},
        UP: {"cells": jnp.minimum(zi + 1, last)},
        DOWN: {"cells": jnp.maximum(zi - 1, 0)},
        ACROSS: {"grow": g_across},
    }
    owner = (zi * 2) // nz == yi
    own_col = pl.multiple_of((zi % (nz // 2)) * rows, rows)
    rest_col = pl.multiple_of(rows - (zi % (nz // 2)) * rows, rows)
    tip = (zi == 0) | (zi == last)
    far_end = jnp.where(zi == 0, last, 0)

    barrier = pltpu.get_barrier_semaphore()

    def greet(to):
        pl.semaphore_signal(barrier, inc=1, device_id=to, device_id_type=MESH)

    peers = [
        {"grow": (gi + dg) % 4, "gcol": (yi + dy) % 2}
        for dg in range(4) for dy in range(2) if dg or dy
    ]
    for peer in peers:
        greet(peer)
    pl.when(zi < last)(lambda: greet(target[UP]))
    pl.when(zi > 0)(lambda: greet(target[DOWN]))
    loads = [
        pltpu.make_async_copy(
            counts_ref.at[pl.ds(cuts[h], cuts[h + 1] - cuts[h]), 0, :],
            staged.at[pl.ds(cuts[h], cuts[h + 1] - cuts[h]), :], load_sem.at[h],
        )
        for h in range(parts)
    ]
    for dma in loads:
        dma.start()

    def part(h):
        return pl.ds(cuts[h], cuts[h + 1] - cuts[h])

    def copy(kind, z, g, h, narrow=False):
        ref = xs.at[z, g, part(h), pl.ds(own_col, rows)] if narrow else xs.at[z, g, part(h), :]
        return pltpu.make_async_remote_copy(
            src_ref=ref, dst_ref=ref,
            send_sem=send_sem.at[kind, z, g // 2, h], recv_sem=recv_sem.at[z, g, h],
            device_id=target[kind], device_id_type=MESH,
        )

    def more_copy(z, h, i):
        return pltpu.make_async_remote_copy(
            src_ref=xs.at[z, g_across, part(h), pl.ds(own_col, rows)],
            dst_ref=xs.at[z, g_across, part(h), pl.ds(rest_col, rows)],
            send_sem=more_send.at[i, h], recv_sem=more_recv.at[i, h],
            device_id={"gcol": 1 - yi}, device_id_type=MESH,
        )

    def answer(i):
        return [
            pltpu.make_async_remote_copy(
                src_ref=src.at[i], dst_ref=dst.at[i],
                send_sem=told_sem.at[i, j], recv_sem=asked_sem.at[i, j],
                device_id=target[ACROSS], device_id_type=MESH,
            )
            for j, (src, dst) in enumerate(((told_unit, asked_unit), (told, asked)))
        ]

    def rows_copy(z, h):
        return pltpu.make_async_remote_copy(
            src_ref=xs.at[z, gi, part(h), pl.ds(own_col, rows)], dst_ref=landed.at[z, part(h), :],
            send_sem=rows_send.at[z, h], recv_sem=rows_recv.at[z, h],
            device_id={"gcol": 1 - yi}, device_id_type=MESH,
        )

    def sends(z, mine, h, act):
        g = gi if mine else g_across
        if mine:
            pl.when((z <= zi) & (zi < last))(lambda: act(copy(UP, z, g, h)))
            pl.when((z >= zi) & (zi > 0))(lambda: act(copy(DOWN, z, g, h)))
            by_line = ((z == 0) & (zi != 0)) | ((z == last) & (zi != last))
            some = tip & (z - zi <= 1) & (zi - z <= 1)
            if h >= m:
                some = some & (z != zi)
            pl.when(some)(lambda: act(copy(ACROSS, z, g, h, True)))
            whole = jnp.logical_not(some)
            if h >= m:
                whole = whole & jnp.logical_not(by_line)
            pl.when(whole)(lambda: act(copy(ACROSS, z, g, h)))
            pl.when(owner)(lambda: act(rows_copy(z, h)))
        elif h >= m:
            pl.when((z == 0) & (zi < last))(lambda: act(copy(UP, z, g, h)))
            pl.when((z == last) & (zi > 0))(lambda: act(copy(DOWN, z, g, h)))
        if mine:
            act(copy(SIB, z, g, h))
        else:
            some = tip & (z - zi <= 1) & (zi - z <= 1)
            if h >= m:
                some = some & (z != zi)
            pl.when(some)(lambda: act(copy(SIB, z, g, h, True)))
            pl.when(jnp.logical_not(some))(lambda: act(copy(SIB, z, g, h)))

    def start(dma):
        dma.start()

    def finish(dma):
        dma.wait_send()

    def arrive(z, g, h, narrow=False):
        copy(SIB, z, g, h, narrow).wait_recv()

    def place(d, side):
        z = zi - d + 2 * d * side
        valid = (z >= 0) & (z <= last) & ((d > 0) | (side == 0))
        return z, valid

    def forward(d):
        for h in range(parts):
            for side in range(2):
                z, valid = place(d, side)

                @pl.when(valid)
                def _():
                    pl.when(d > 0)(lambda: arrive(z, gi, h))
                    sends(z, True, h, start)

    def ends(d):
        for z, hit in ((0, zi == d - 1), (last, last - zi == d - 1)):
            @pl.when(hit)
            def _():
                for h in range(m, parts):
                    arrive(z, g_across, h)
                    sends(z, False, h, start)

    def turn(z, g, into, first, end, there):
        def body(k, carry):
            r = pl.ds(pl.multiple_of(k * 128, 128), 128)

            @pl.when(owner)
            def _():
                turned[into, :, r] = xs[z, g, r, pl.ds(own_col, rows)].T

            @pl.when(jnp.logical_not(owner))
            def _():
                turned[into, :, r] = there(r).T
            return carry

        lax.fori_loop(first // 128, end // 128, body, 0)

    def multiply(z, g, lo, hi, both=False, col=0, wide=None, theirs=False):
        tiles = (wide or width) // TILE

        def body(i, carry):
            a = (g // 2) * 2 + (g + i // tiles) % 2
            n = pl.ds(pl.multiple_of(col + (i % tiles) * TILE, TILE), TILE)
            into, left = (a + 2) % 4 if theirs else a, far_end if theirs else z
            acc[into, :, n] += jnp.dot(
                turned[left, :, lo:hi], xs[z, a, lo:hi, n], preferred_element_type=jnp.float32
            )
            return carry

        lax.fori_loop(0, tiles * (2 if both else 1), body, 0)

    def near(d):
        def body(side, carry):
            z, valid = place(d, side)

            @pl.when(valid)
            def _():
                @pl.when(jnp.logical_not(owner))
                def _():
                    for h in range(parts):
                        rows_copy(z, h).wait_recv()

                turn(z, gi, z, 0, cuts[-1], lambda r: landed[z, r, :])
                for h in range(parts):
                    arrive(z, g_sib, h)
                multiply(z, gi, 0, cuts[-1], both=True)
            return carry

        lax.fori_loop(0, 2, body, 0)

    def deliver(a):
        def scale(k, carry):
            r = pl.ds(pl.multiple_of(k * 64, 64), 64)
            acc[a, r, :] = acc[a, r, :] * (1.0 / (nz * cuts[-1]))
            return carry

        lax.fori_loop(0, rows // 64, scale, 0)
        pltpu.make_async_copy(acc.at[a], out_ref.at[:, a, :], out_sem.at[a]).start()

    def tip_far(z, d):
        def each(h, act):
            act(h) if h < m else pl.when(d == 1)(lambda: act(h))

        def take(h):
            arrive(z, g_across, h, True)
            start(copy(SIB, z, g_across, h, True))
            pl.when(owner)(lambda: more_copy(z, h, d).start())

        for h in range(parts):
            each(h, take)
        def wait_more(h):
            pl.when(jnp.logical_not(owner))(lambda: more_copy(z, h, d).wait_recv())

        for h in range(parts):
            each(h, wait_more)

        def theirs(lo, hi):
            turn(z, g_across, far_end, lo, hi, lambda r: xs[z, g_across, r, pl.ds(rest_col, rows)])
            multiply(z, gi, lo, hi, True, rest_col, rows, True)

        theirs(0, cuts[m])

        @pl.when(d == 1)
        def _():
            theirs(cuts[m], cuts[-1])
            for i, a in enumerate((g_across, g_other)):
                def code(j, carry):
                    col = pl.ds(pl.multiple_of(rest_col + j * 128, 128), 128)
                    at = pl.ds(pl.multiple_of(j * 128, 128), 128)
                    sent = acc[a, :, col]
                    top = jnp.maximum(jnp.max(jnp.abs(sent), axis=0, keepdims=True), 1e-30)
                    whole = jnp.floor(sent * (LEVELS / top) + 0.5).astype(jnp.int32)
                    told[i, :, at] = whole.astype(jnp.int16)
                    told_unit[i, :, at] = jnp.broadcast_to(top * (1.0 / LEVELS), (8, 128))
                    acc[a, :, col] = jnp.zeros((rows, 128), jnp.float32)
                    return carry

                lax.fori_loop(0, rows // 128, code, 0)
                for dma in answer(i):
                    dma.start()

        for h in range(parts):
            if h < m:
                arrive(z, g_other, h, True)
            else:
                pl.when(d == 1)(lambda: arrive(z, g_other, h, True))
                pl.when(d == 0)(lambda: arrive(z, g_other, h))
        multiply(z, g_across, 0, cuts[-1], True, own_col, rows)

        @pl.when(d == 1)
        def _():
            multiply(zi, g_across, cuts[m], cuts[-1], True, rest_col, rows)

    def far(d):
        def body(side, carry):
            z, valid = place(d, side)
            at_end = (z == 0) | (z == last)

            def take(h):
                arrive(z, g_across, h)
                start(copy(SIB, z, g_across, h))

            @pl.when(valid & tip & (d <= 1))
            def _():
                tip_far(z, d)

            @pl.when(valid & jnp.logical_not(at_end) & jnp.logical_not(tip & (d <= 1)))
            def _():
                for h in range(parts):
                    take(h)
                for h in range(parts):
                    arrive(z, g_other, h)
                multiply(z, g_across, 0, cuts[-1], both=True)

            @pl.when(valid & at_end & jnp.logical_not(tip & (d <= 1)))
            def _():
                order = sorted(range(parts), key=lambda h: (h - m + 0.5 if h >= m else h))
                for h in order:
                    if h < m:
                        take(h)
                    else:
                        pl.when(d == last)(lambda: take(h))
                    if h != order[-1]:
                        arrive(z, g_other, h)
                        multiply(z, g_across, cuts[h], cuts[h + 1], both=True)
                    else:
                        multiply(z, g_across, cuts[h], cuts[h + 1])
                        pl.when(d == last)(lambda: deliver(g_across))
                        arrive(z, g_other, h)
                        multiply(z, g_other, cuts[h], cuts[h + 1])
            return carry

        lax.fori_loop(0, 2, body, 0)

    def add_up(k, carry):
        r = pl.ds(pl.multiple_of(k * 128, 128), 128)
        total = staged[r, 0:128].astype(jnp.float32)
        for j in range(128, width, 128):
            total += staged[r, j:j + 128].astype(jnp.float32)
        sums[pl.ds(k, 1), :] = jnp.sum(total.T, axis=0, keepdims=True)
        return carry

    def standardize_rows(k, carry):
        r = pl.ds(pl.multiple_of(k * 128, 128), 128)
        share = GENES / jnp.broadcast_to(sums[pl.ds(k, 1), :], (128, 128)).T
        for j in range(0, width, 128):
            lognorm = jnp.log1p(staged[r, j:j + 128].astype(jnp.float32) * share)
            xs[zi, gi, r, j:j + 128] = (
                (lognorm - mean_ref[:, j:j + 128]) / scale_ref[:, j:j + 128]
            ).astype(jnp.bfloat16)
        return carry

    sums[...] = jnp.zeros_like(sums)
    for h in range(parts):
        loads[h].wait()
        lax.fori_loop(cuts[h] // 128, cuts[h + 1] // 128, add_up, 0)
    ends_of_line = (zi == 0).astype(jnp.int32) + (zi == last).astype(jnp.int32)
    pl.semaphore_wait(barrier, len(peers) + 2 - ends_of_line)
    tells = [
        pltpu.make_async_remote_copy(
            src_ref=sums, dst_ref=heard.at[i], send_sem=sums_send.at[i], recv_sem=sums_recv.at[i],
            device_id=peer, device_id_type=MESH,
        )
        for i, peer in enumerate(peers)
    ]
    for dma in tells:
        dma.start()
    for dma in tells:
        dma.wait()
    whole = sums[...]
    for i in range(len(peers)):
        whole += heard[i]
    sums[...] = whole
    for h in range(parts):
        lax.fori_loop(cuts[h] // 128, cuts[h + 1] // 128, standardize_rows, 0)
        sends(zi, True, h, start)

    def clear(k, carry):
        acc[k // 8, pl.ds((k % 8) * (rows // 8), rows // 8), :] = jnp.zeros(
            (rows // 8, width), jnp.float32)
        return carry

    lax.fori_loop(0, acc.shape[0] * 8, clear, 0)

    def step(d, carry):
        @pl.when(d == nz)
        def _():
            deliver(gi)
            deliver(g_sib)

            @pl.when(tip)
            def _():
                for i, a in enumerate((g_across, g_other)):
                    for dma in answer(i):
                        dma.wait()
                    def decode(j, carry):
                        col = pl.ds(pl.multiple_of(rest_col + j * 128, 128), 128)
                        at = pl.ds(pl.multiple_of(j * 128, 128), 128)
                        got = asked[i, :, at].astype(jnp.int32).astype(jnp.float32)
                        acc[a, :, col] += got * asked_unit[i, 0:1, at]
                        return carry

                    lax.fori_loop(0, rows // 128, decode, 0)

        pl.when((d > 0) & (d < nz))(lambda: forward(d))
        pl.when(d < nz)(lambda: ends(d))
        pl.when(d < nz)(lambda: near(d))
        pl.when(d > 0)(lambda: far(d - 1))
        return carry

    lax.fori_loop(0, nz + 1, step, 0)
    pl.when((zi > 0) & (zi < last))(lambda: deliver(g_across))
    deliver(g_other)

    def drain(z, carry):
        for h in range(parts):
            for mine in (True, False):
                sends(z, mine, h, finish)
        return carry

    lax.fori_loop(0, nz, drain, 0)

    @pl.when(tip & owner)
    def _():
        for h in range(parts):
            if h < m:
                more_copy(zi, h, 0).wait_send()
            more_copy(jnp.where(zi == 0, 1, last - 1), h, 1).wait_send()

    for a in range(acc.shape[0]):
        pltpu.make_async_copy(acc.at[a], out_ref.at[:, a, :], out_sem.at[a]).wait()


def copy_kernel(src, dst, held, load_sems, store_sems):
    n = load_sems.shape[0]
    each = src.shape[0] // n
    at = [pl.ds(i * each, each) for i in range(n)]
    loads = [pltpu.make_async_copy(src.at[r], held.at[r], load_sems.at[i]) for i, r in enumerate(at)]
    stores = [pltpu.make_async_copy(held.at[r], dst.at[r], store_sems.at[i]) for i, r in enumerate(at)]
    for dma in loads:
        dma.start()
    for load, store in zip(loads, stores):
        load.wait()
        store.start()
    for dma in stores:
        dma.wait()


def line_plan(counts, gene_mean, gene_scale):
    nz, n_grow = lax.axis_size("cells"), lax.axis_size("grow")
    cell_rows, width = counts.shape[0], counts.shape[3]
    rows = 2 * width // nz
    cuts, m = (0, 384, 640, 768, 1024, cell_rows), 3
    flops = 2 * rows * n_grow * width * nz * cell_rows
    scaled = pl.pallas_call(
        functools.partial(gram_kernel, nz, rows, cuts, m),
        out_shape=jax.ShapeDtypeStruct((rows, n_grow, width), jnp.float32),
        in_specs=[
            pl.BlockSpec(memory_space=pl.ANY),
            pl.BlockSpec(memory_space=pltpu.VMEM),
            pl.BlockSpec(memory_space=pltpu.VMEM),
        ],
        out_specs=pl.BlockSpec(memory_space=pl.ANY),
        scratch_shapes=[
            pltpu.VMEM((cell_rows, width), jnp.int32),
            pltpu.VMEM((-(-cell_rows // 1024) * 8, 128), jnp.float32),
            pltpu.VMEM((7, -(-cell_rows // 1024) * 8, 128), jnp.float32),
            pltpu.VMEM((nz, n_grow, cell_rows, width), jnp.bfloat16),
            pltpu.VMEM((nz, cell_rows, rows), jnp.bfloat16),
            pltpu.VMEM((nz, rows, cell_rows), jnp.bfloat16),
            pltpu.VMEM((n_grow, rows, width), jnp.float32),
            pltpu.VMEM((2, rows, rows), jnp.int16),
            pltpu.VMEM((2, rows, rows), jnp.int16),
            pltpu.VMEM((2, 8, rows), jnp.float32),
            pltpu.VMEM((2, 8, rows), jnp.float32),
            pltpu.SemaphoreType.DMA((len(cuts) - 1,)),
            pltpu.SemaphoreType.DMA((7,)),
            pltpu.SemaphoreType.DMA((7,)),
            pltpu.SemaphoreType.DMA((nz, n_grow, len(cuts) - 1)),
            pltpu.SemaphoreType.DMA((4, nz, 2, len(cuts) - 1)),
            pltpu.SemaphoreType.DMA((nz, len(cuts) - 1)),
            pltpu.SemaphoreType.DMA((nz, len(cuts) - 1)),
            pltpu.SemaphoreType.DMA((n_grow,)),
            pltpu.SemaphoreType.DMA((2, len(cuts) - 1)),
            pltpu.SemaphoreType.DMA((2, len(cuts) - 1)),
            pltpu.SemaphoreType.DMA((2, 2)),
            pltpu.SemaphoreType.DMA((2, 2)),
        ],
        compiler_params=pltpu.CompilerParams(
            collective_id=0, has_side_effects=True, vmem_limit_bytes=63 * 2**20
        ),
        cost_estimate=pl.CostEstimate(
            flops=flops, bytes_accessed=4 * rows * n_grow * width, transcendentals=0
        ),
    )(counts.reshape(cell_rows, 1, width), gene_mean.reshape(1, width), gene_scale.reshape(1, width))
    copied = pl.pallas_call(
        copy_kernel,
        out_shape=jax.ShapeDtypeStruct(scaled.shape, scaled.dtype),
        in_specs=[pl.BlockSpec(memory_space=pl.ANY)],
        out_specs=pl.BlockSpec(memory_space=pl.ANY),
        scratch_shapes=[
            pltpu.VMEM(scaled.shape, scaled.dtype),
            pltpu.SemaphoreType.DMA((16,)),
            pltpu.SemaphoreType.DMA((16,)),
        ],
        compiler_params=pltpu.CompilerParams(vmem_limit_bytes=62 * 2**20),
    )(scaled)
    return copied.reshape(1, rows, 1, n_grow, width)


def sum_plan(counts, gene_mean, gene_scale):
    cell_rows, width = counts.shape[0], counts.shape[3]
    standard = standardize(counts, gene_mean, gene_scale).reshape(cell_rows, 1, width)
    n_grow, n_gcol, n_cells = (lax.axis_size(a) for a in ("grow", "gcol", "cells"))
    row_flat = lax.all_gather(standard, "gcol", axis=1, tiled=True).reshape(cell_rows, -1)
    col_flat = lax.all_gather(standard, "grow", axis=1, tiled=True).reshape(cell_rows, -1)
    owned = row_flat.shape[1] // n_cells
    summed = lax.psum_scatter(
        lax.dot_general(
            row_flat, col_flat, (((0,), (0,)), ((), ())), preferred_element_type=jnp.float32
        ),
        "cells",
        scatter_dimension=0,
        tiled=True,
    )
    return (summed / (n_cells * cell_rows)).reshape(1, owned, 1, n_grow, width)


def solution(mesh):
    placed = (P("cells", "grow", "gcol", None), P("grow", "gcol", None), P("grow", "gcol", None))
    sizes = tuple(mesh.shape[a] for a in ("cells", "grow", "gcol"))
    return jax.shard_map(
        line_plan if sizes == (4, 4, 2) else sum_plan,
        mesh=mesh,
        in_specs=placed,
        out_specs=P("grow", "cells", "gcol", None, None),
        check_vma=False,
    )
```

```python
import functools

import jax
import jax.numpy as jnp
from jax import lax
from jax.experimental import pallas as pl
from jax.experimental.pallas import tpu as pltpu
from jax.sharding import PartitionSpec as P

GENES = 8192
MESH = pl.DeviceIdType.MESH
SIB, UP, DOWN, ACROSS = range(4)
TILE = 256
LEVELS = 32767.0


def standardize(counts, gene_mean, gene_scale):
    cell_rows, width = counts.shape[0], counts.shape[3]
    local = counts.reshape(cell_rows, width).astype(jnp.float32)
    totals = lax.psum(jnp.sum(local, axis=1), ("grow", "gcol"))
    lognorm = jnp.log1p(local * GENES / totals[:, None])
    return ((lognorm - gene_mean.reshape(1, width)) / gene_scale.reshape(1, width)).astype(
        jnp.bfloat16
    )


def gram_kernel(nz, rows, cuts, m, counts_ref, mean_ref, scale_ref, out_ref,
                staged, sums, heard, xs, landed, turned, acc, told, asked, told_unit, asked_unit,
                load_sem, sums_recv, sums_send, recv_sem, send_sem, rows_recv, rows_send, out_sem,
                more_recv, more_send, asked_sem, told_sem):
    zi, gi, yi = lax.axis_index("cells"), lax.axis_index("grow"), lax.axis_index("gcol")
    width = xs.shape[3]
    last = nz - 1
    parts = len(cuts) - 1
    x, c = gi // 2, gi % 2
    g_sib = x * 2 + (1 - c)
    g_across = (1 - x) * 2 + c
    g_other = (1 - x) * 2 + (1 - c)
    target = {
        SIB: {"grow": g_sib},
        UP: {"cells": jnp.minimum(zi + 1, last)},
        DOWN: {"cells": jnp.maximum(zi - 1, 0)},
        ACROSS: {"grow": g_across},
    }
    owner = (zi * 2) // nz == yi
    own_col = pl.multiple_of((zi % (nz // 2)) * rows, rows)
    rest_col = pl.multiple_of(rows - (zi % (nz // 2)) * rows, rows)
    tip = (zi == 0) | (zi == last)
    far_end = jnp.where(zi == 0, last, 0)

    barrier = pltpu.get_barrier_semaphore()

    def greet(to):
        pl.semaphore_signal(barrier, inc=1, device_id=to, device_id_type=MESH)

    peers = [
        {"grow": (gi + dg) % 4, "gcol": (yi + dy) % 2}
        for dg in range(4) for dy in range(2) if dg or dy
    ]
    for peer in peers:
        greet(peer)
    pl.when(zi < last)(lambda: greet(target[UP]))
    pl.when(zi > 0)(lambda: greet(target[DOWN]))
    loads = [
        pltpu.make_async_copy(
            counts_ref.at[pl.ds(cuts[h], cuts[h + 1] - cuts[h]), 0, :],
            staged.at[pl.ds(cuts[h], cuts[h + 1] - cuts[h]), :], load_sem.at[h],
        )
        for h in range(parts)
    ]
    for dma in loads:
        dma.start()

    def part(h):
        return pl.ds(cuts[h], cuts[h + 1] - cuts[h])

    def copy(kind, z, g, h, narrow=False):
        ref = xs.at[z, g, part(h), pl.ds(own_col, rows)] if narrow else xs.at[z, g, part(h), :]
        return pltpu.make_async_remote_copy(
            src_ref=ref, dst_ref=ref,
            send_sem=send_sem.at[kind, z, g // 2, h], recv_sem=recv_sem.at[z, g, h],
            device_id=target[kind], device_id_type=MESH,
        )

    def more_copy(z, h, i):
        return pltpu.make_async_remote_copy(
            src_ref=xs.at[z, g_across, part(h), pl.ds(own_col, rows)],
            dst_ref=xs.at[z, g_across, part(h), pl.ds(rest_col, rows)],
            send_sem=more_send.at[i, h], recv_sem=more_recv.at[i, h],
            device_id={"gcol": 1 - yi}, device_id_type=MESH,
        )

    def answer(i):
        return [
            pltpu.make_async_remote_copy(
                src_ref=src.at[i], dst_ref=dst.at[i],
                send_sem=told_sem.at[i, j], recv_sem=asked_sem.at[i, j],
                device_id=target[ACROSS], device_id_type=MESH,
            )
            for j, (src, dst) in enumerate(((told_unit, asked_unit), (told, asked)))
        ]

    def rows_copy(z, h):
        return pltpu.make_async_remote_copy(
            src_ref=xs.at[z, gi, part(h), pl.ds(own_col, rows)], dst_ref=landed.at[z, part(h), :],
            send_sem=rows_send.at[z, h], recv_sem=rows_recv.at[z, h],
            device_id={"gcol": 1 - yi}, device_id_type=MESH,
        )

    def sends(z, mine, h, act):
        g = gi if mine else g_across
        if mine:
            pl.when((z <= zi) & (zi < last))(lambda: act(copy(UP, z, g, h)))
            pl.when((z >= zi) & (zi > 0))(lambda: act(copy(DOWN, z, g, h)))
            by_line = ((z == 0) & (zi != 0)) | ((z == last) & (zi != last))
            some = tip & (z - zi <= 1) & (zi - z <= 1)
            if h >= m:
                some = some & (z != zi)
            pl.when(some)(lambda: act(copy(ACROSS, z, g, h, True)))
            whole = jnp.logical_not(some)
            if h >= m:
                whole = whole & jnp.logical_not(by_line)
            pl.when(whole)(lambda: act(copy(ACROSS, z, g, h)))
            pl.when(owner)(lambda: act(rows_copy(z, h)))
        elif h >= m:
            pl.when((z == 0) & (zi < last))(lambda: act(copy(UP, z, g, h)))
            pl.when((z == last) & (zi > 0))(lambda: act(copy(DOWN, z, g, h)))
        if mine:
            act(copy(SIB, z, g, h))
        else:
            some = tip & (z - zi <= 1) & (zi - z <= 1)
            if h >= m:
                some = some & (z != zi)
            pl.when(some)(lambda: act(copy(SIB, z, g, h, True)))
            pl.when(jnp.logical_not(some))(lambda: act(copy(SIB, z, g, h)))

    def start(dma):
        dma.start()

    def finish(dma):
        dma.wait_send()

    def arrive(z, g, h, narrow=False):
        copy(SIB, z, g, h, narrow).wait_recv()

    def place(d, side):
        z = zi - d + 2 * d * side
        valid = (z >= 0) & (z <= last) & ((d > 0) | (side == 0))
        return z, valid

    def forward(d):
        for h in range(parts):
            for side in range(2):
                z, valid = place(d, side)

                @pl.when(valid)
                def _():
                    pl.when(d > 0)(lambda: arrive(z, gi, h))
                    sends(z, True, h, start)

    def ends(d):
        for z, hit in ((0, zi == d - 1), (last, last - zi == d - 1)):
            @pl.when(hit)
            def _():
                for h in range(m, parts):
                    arrive(z, g_across, h)
                    sends(z, False, h, start)

    def turn(z, g, into, first, end, there):
        def body(k, carry):
            r = pl.ds(pl.multiple_of(k * 128, 128), 128)

            @pl.when(owner)
            def _():
                turned[into, :, r] = xs[z, g, r, pl.ds(own_col, rows)].T

            @pl.when(jnp.logical_not(owner))
            def _():
                turned[into, :, r] = there(r).T
            return carry

        lax.fori_loop(first // 128, end // 128, body, 0)

    def multiply(z, g, lo, hi, both=False, col=0, wide=None, theirs=False):
        tiles = (wide or width) // TILE

        def body(i, carry):
            a = (g // 2) * 2 + (g + i // tiles) % 2
            n = pl.ds(pl.multiple_of(col + (i % tiles) * TILE, TILE), TILE)
            into, left = (a + 2) % 4 if theirs else a, far_end if theirs else z
            acc[into, :, n] += jnp.dot(
                turned[left, :, lo:hi], xs[z, a, lo:hi, n], preferred_element_type=jnp.float32
            )
            return carry

        lax.fori_loop(0, tiles * (2 if both else 1), body, 0)

    def near(d):
        def body(side, carry):
            z, valid = place(d, side)

            @pl.when(valid)
            def _():
                @pl.when(jnp.logical_not(owner))
                def _():
                    for h in range(parts):
                        rows_copy(z, h).wait_recv()

                turn(z, gi, z, 0, cuts[-1], lambda r: landed[z, r, :])
                for h in range(parts):
                    arrive(z, g_sib, h)
                multiply(z, gi, 0, cuts[-1], both=True)
            return carry

        lax.fori_loop(0, 2, body, 0)

    def deliver(a):
        def scale(k, carry):
            r = pl.ds(pl.multiple_of(k * 64, 64), 64)
            acc[a, r, :] = acc[a, r, :] * (1.0 / (nz * cuts[-1]))
            return carry

        lax.fori_loop(0, rows // 64, scale, 0)
        pltpu.make_async_copy(acc.at[a], out_ref.at[:, a, :], out_sem.at[a]).start()

    def each(h, d, act):
        act(h) if h < m else pl.when(d == 1)(lambda: act(h))

    def tip_take(d):
        z = jnp.where(zi == 0, d, last - d)

        def take(h):
            arrive(z, g_across, h, True)
            start(copy(SIB, z, g_across, h, True))
            pl.when(owner)(lambda: more_copy(z, h, d).start())

        for h in range(parts):
            each(h, d, take)

    def tip_far(z, d):
        def wait_more(h):
            pl.when(jnp.logical_not(owner))(lambda: more_copy(z, h, d).wait_recv())

        for h in range(parts):
            each(h, d, wait_more)

        def theirs(lo, hi):
            turn(z, g_across, far_end, lo, hi, lambda r: xs[z, g_across, r, pl.ds(rest_col, rows)])
            multiply(z, gi, lo, hi, True, rest_col, rows, True)

        theirs(0, cuts[m])

        @pl.when(d == 1)
        def _():
            theirs(cuts[m], cuts[-1])
            for i, a in enumerate((g_across, g_other)):
                def code(j, carry):
                    col = pl.ds(pl.multiple_of(rest_col + j * 128, 128), 128)
                    at = pl.ds(pl.multiple_of(j * 128, 128), 128)
                    sent = acc[a, :, col]
                    top = jnp.maximum(jnp.max(jnp.abs(sent), axis=0, keepdims=True), 1e-30)
                    whole = jnp.floor(sent * (LEVELS / top) + 0.5).astype(jnp.int32)
                    told[i, :, at] = whole.astype(jnp.int16)
                    told_unit[i, :, at] = jnp.broadcast_to(top * (1.0 / LEVELS), (8, 128))
                    acc[a, :, col] = jnp.zeros((rows, 128), jnp.float32)
                    return carry

                lax.fori_loop(0, rows // 128, code, 0)
                for dma in answer(i):
                    dma.start()

        for h in range(parts):
            if h < m:
                arrive(z, g_other, h, True)
            else:
                pl.when(d == 1)(lambda: arrive(z, g_other, h, True))
                pl.when(d == 0)(lambda: arrive(z, g_other, h))
        multiply(z, g_across, 0, cuts[-1], True, own_col, rows)

        @pl.when(d == 1)
        def _():
            multiply(zi, g_across, cuts[m], cuts[-1], True, rest_col, rows)

    def far(d):
        def body(side, carry):
            z, valid = place(d, side)
            at_end = (z == 0) | (z == last)

            def take(h):
                arrive(z, g_across, h)
                start(copy(SIB, z, g_across, h))

            @pl.when(valid & tip & (d <= 1))
            def _():
                tip_far(z, d)

            @pl.when(valid & jnp.logical_not(at_end) & jnp.logical_not(tip & (d <= 1)))
            def _():
                for h in range(parts):
                    take(h)
                for h in range(parts):
                    arrive(z, g_other, h)
                multiply(z, g_across, 0, cuts[-1], both=True)

            @pl.when(valid & at_end & jnp.logical_not(tip & (d <= 1)))
            def _():
                order = sorted(range(parts), key=lambda h: (h - m + 0.5 if h >= m else h))
                for h in order:
                    if h < m:
                        take(h)
                    else:
                        pl.when(d == last)(lambda: take(h))
                    if h != order[-1]:
                        arrive(z, g_other, h)
                        multiply(z, g_across, cuts[h], cuts[h + 1], both=True)
                    else:
                        multiply(z, g_across, cuts[h], cuts[h + 1])
                        pl.when(d == last)(lambda: deliver(g_across))
                        arrive(z, g_other, h)
                        multiply(z, g_other, cuts[h], cuts[h + 1])
            return carry

        lax.fori_loop(0, 2, body, 0)

    def add_up(k, carry):
        r = pl.ds(pl.multiple_of(k * 128, 128), 128)
        total = staged[r, 0:128].astype(jnp.float32)
        for j in range(128, width, 128):
            total += staged[r, j:j + 128].astype(jnp.float32)
        sums[pl.ds(k, 1), :] = jnp.sum(total.T, axis=0, keepdims=True)
        return carry

    def standardize_rows(k, carry):
        r = pl.ds(pl.multiple_of(k * 128, 128), 128)
        share = GENES / jnp.broadcast_to(sums[pl.ds(k, 1), :], (128, 128)).T
        for j in range(0, width, 128):
            lognorm = jnp.log1p(staged[r, j:j + 128].astype(jnp.float32) * share)
            xs[zi, gi, r, j:j + 128] = (
                (lognorm - mean_ref[:, j:j + 128]) / scale_ref[:, j:j + 128]
            ).astype(jnp.bfloat16)
        return carry

    sums[...] = jnp.zeros_like(sums)
    for h in range(parts):
        loads[h].wait()
        lax.fori_loop(cuts[h] // 128, cuts[h + 1] // 128, add_up, 0)
    ends_of_line = (zi == 0).astype(jnp.int32) + (zi == last).astype(jnp.int32)
    pl.semaphore_wait(barrier, len(peers) + 2 - ends_of_line)
    tells = [
        pltpu.make_async_remote_copy(
            src_ref=sums, dst_ref=heard.at[i], send_sem=sums_send.at[i], recv_sem=sums_recv.at[i],
            device_id=peer, device_id_type=MESH,
        )
        for i, peer in enumerate(peers)
    ]
    for dma in tells:
        dma.start()
    for dma in tells:
        dma.wait()
    whole = sums[...]
    for i in range(len(peers)):
        whole += heard[i]
    sums[...] = whole
    for h in range(parts):
        lax.fori_loop(cuts[h] // 128, cuts[h + 1] // 128, standardize_rows, 0)
        sends(zi, True, h, start)

    def clear(k, carry):
        acc[k // 8, pl.ds((k % 8) * (rows // 8), rows // 8), :] = jnp.zeros(
            (rows // 8, width), jnp.float32)
        return carry

    lax.fori_loop(0, acc.shape[0] * 8, clear, 0)

    def step(d, carry):
        @pl.when(d == nz)
        def _():
            deliver(gi)
            deliver(g_sib)

            @pl.when(tip)
            def _():
                for i, a in enumerate((g_across, g_other)):
                    for dma in answer(i):
                        dma.wait()
                    def decode(j, carry):
                        col = pl.ds(pl.multiple_of(rest_col + j * 128, 128), 128)
                        at = pl.ds(pl.multiple_of(j * 128, 128), 128)
                        got = asked[i, :, at].astype(jnp.int32).astype(jnp.float32)
                        acc[a, :, col] += got * asked_unit[i, 0:1, at]
                        return carry

                    lax.fori_loop(0, rows // 128, decode, 0)

        pl.when((d > 0) & (d < nz))(lambda: forward(d))
        pl.when(d < nz)(lambda: ends(d))
        pl.when(d > 0)(lambda: far(d - 1))
        pl.when(d < nz)(lambda: near(d))
        pl.when(tip & (d < 2))(lambda: tip_take(d))
        return carry

    lax.fori_loop(0, nz + 1, step, 0)
    pl.when((zi > 0) & (zi < last))(lambda: deliver(g_across))
    deliver(g_other)

    def drain(z, carry):
        for h in range(parts):
            for mine in (True, False):
                sends(z, mine, h, finish)
        return carry

    lax.fori_loop(0, nz, drain, 0)

    @pl.when(tip & owner)
    def _():
        for h in range(parts):
            if h < m:
                more_copy(zi, h, 0).wait_send()
            more_copy(jnp.where(zi == 0, 1, last - 1), h, 1).wait_send()

    for a in range(acc.shape[0]):
        pltpu.make_async_copy(acc.at[a], out_ref.at[:, a, :], out_sem.at[a]).wait()


def copy_kernel(src, dst, held, load_sems, store_sems):
    n = load_sems.shape[0]
    each = src.shape[0] // n
    at = [pl.ds(i * each, each) for i in range(n)]
    loads = [pltpu.make_async_copy(src.at[r], held.at[r], load_sems.at[i]) for i, r in enumerate(at)]
    stores = [pltpu.make_async_copy(held.at[r], dst.at[r], store_sems.at[i]) for i, r in enumerate(at)]
    for dma in loads:
        dma.start()
    for load, store in zip(loads, stores):
        load.wait()
        store.start()
    for dma in stores:
        dma.wait()


def line_plan(counts, gene_mean, gene_scale):
    nz, n_grow = lax.axis_size("cells"), lax.axis_size("grow")
    cell_rows, width = counts.shape[0], counts.shape[3]
    rows = 2 * width // nz
    cuts, m = (0, 384, 640, 768, 1024, cell_rows), 3
    flops = 2 * rows * n_grow * width * nz * cell_rows
    scaled = pl.pallas_call(
        functools.partial(gram_kernel, nz, rows, cuts, m),
        out_shape=jax.ShapeDtypeStruct((rows, n_grow, width), jnp.float32),
        in_specs=[
            pl.BlockSpec(memory_space=pl.ANY),
            pl.BlockSpec(memory_space=pltpu.VMEM),
            pl.BlockSpec(memory_space=pltpu.VMEM),
        ],
        out_specs=pl.BlockSpec(memory_space=pl.ANY),
        scratch_shapes=[
            pltpu.VMEM((cell_rows, width), jnp.int32),
            pltpu.VMEM((-(-cell_rows // 1024) * 8, 128), jnp.float32),
            pltpu.VMEM((7, -(-cell_rows // 1024) * 8, 128), jnp.float32),
            pltpu.VMEM((nz, n_grow, cell_rows, width), jnp.bfloat16),
            pltpu.VMEM((nz, cell_rows, rows), jnp.bfloat16),
            pltpu.VMEM((nz, rows, cell_rows), jnp.bfloat16),
            pltpu.VMEM((n_grow, rows, width), jnp.float32),
            pltpu.VMEM((2, rows, rows), jnp.int16),
            pltpu.VMEM((2, rows, rows), jnp.int16),
            pltpu.VMEM((2, 8, rows), jnp.float32),
            pltpu.VMEM((2, 8, rows), jnp.float32),
            pltpu.SemaphoreType.DMA((len(cuts) - 1,)),
            pltpu.SemaphoreType.DMA((7,)),
            pltpu.SemaphoreType.DMA((7,)),
            pltpu.SemaphoreType.DMA((nz, n_grow, len(cuts) - 1)),
            pltpu.SemaphoreType.DMA((4, nz, 2, len(cuts) - 1)),
            pltpu.SemaphoreType.DMA((nz, len(cuts) - 1)),
            pltpu.SemaphoreType.DMA((nz, len(cuts) - 1)),
            pltpu.SemaphoreType.DMA((n_grow,)),
            pltpu.SemaphoreType.DMA((2, len(cuts) - 1)),
            pltpu.SemaphoreType.DMA((2, len(cuts) - 1)),
            pltpu.SemaphoreType.DMA((2, 2)),
            pltpu.SemaphoreType.DMA((2, 2)),
        ],
        compiler_params=pltpu.CompilerParams(
            collective_id=0, has_side_effects=True, vmem_limit_bytes=63 * 2**20
        ),
        cost_estimate=pl.CostEstimate(
            flops=flops, bytes_accessed=4 * rows * n_grow * width, transcendentals=0
        ),
    )(counts.reshape(cell_rows, 1, width), gene_mean.reshape(1, width), gene_scale.reshape(1, width))
    copied = pl.pallas_call(
        copy_kernel,
        out_shape=jax.ShapeDtypeStruct(scaled.shape, scaled.dtype),
        in_specs=[pl.BlockSpec(memory_space=pl.ANY)],
        out_specs=pl.BlockSpec(memory_space=pl.ANY),
        scratch_shapes=[
            pltpu.VMEM(scaled.shape, scaled.dtype),
            pltpu.SemaphoreType.DMA((16,)),
            pltpu.SemaphoreType.DMA((16,)),
        ],
        compiler_params=pltpu.CompilerParams(vmem_limit_bytes=62 * 2**20),
    )(scaled)
    return copied.reshape(1, rows, 1, n_grow, width)


def sum_plan(counts, gene_mean, gene_scale):
    cell_rows, width = counts.shape[0], counts.shape[3]
    standard = standardize(counts, gene_mean, gene_scale).reshape(cell_rows, 1, width)
    n_grow, n_gcol, n_cells = (lax.axis_size(a) for a in ("grow", "gcol", "cells"))
    row_flat = lax.all_gather(standard, "gcol", axis=1, tiled=True).reshape(cell_rows, -1)
    col_flat = lax.all_gather(standard, "grow", axis=1, tiled=True).reshape(cell_rows, -1)
    owned = row_flat.shape[1] // n_cells
    summed = lax.psum_scatter(
        lax.dot_general(
            row_flat, col_flat, (((0,), (0,)), ((), ())), preferred_element_type=jnp.float32
        ),
        "cells",
        scatter_dimension=0,
        tiled=True,
    )
    return (summed / (n_cells * cell_rows)).reshape(1, owned, 1, n_grow, width)


def solution(mesh):
    placed = (P("cells", "grow", "gcol", None), P("grow", "gcol", None), P("grow", "gcol", None))
    sizes = tuple(mesh.shape[a] for a in ("cells", "grow", "gcol"))
    return jax.shard_map(
        line_plan if sizes == (4, 4, 2) else sum_plan,
        mesh=mesh,
        in_specs=placed,
        out_specs=P("grow", "cells", "gcol", None, None),
        check_vma=False,
    )
```
